32 devices in a mesh: row: 2 (over x), col: 16 (over z, y, core).
Axes of the slice: x: 2, y: 2, z: 4, core: 2. Of those that a mesh axis runs over, the one named last changes fastest.
Arguments:
- sigma_anc: bfloat16 [4096, 4096], P('row', 'col'), as said below
- top_panel: bfloat16 [4096, 4096], P('row', 'col'), may hold values from -0.09375 to 0.09375
- top_dinv: bfloat16 [4096, 4096], P('row', 'col'), as said below
- low_upper: bfloat16 [4096, 4096], P('row', 'col'), may hold values from -0.09375 to 0.09375
- low_ancestor: bfloat16 [4096, 4096], P('row', 'col'), may hold values from -0.09375 to 0.09375
- low_dinv: bfloat16 [4096, 4096], P('row', 'col'), as said below
- low_rows: int32 [16], replicated, may hold values from 0 to 31, as said below
Outputs:
- top_off: bfloat16 [4096, 4096], P('row', 'col')
- top_diag: bfloat16 [4096, 4096], P('row', 'col')
- low_top: bfloat16 [4096, 4096], P('row', 'col')
- low_anc: bfloat16 [4096, 4096], P('row', 'col')
- low_diag: bfloat16 [4096, 4096], P('row', 'col')
The draws below stay inside these ranges and needn't reach their ends.
Inputs may be any that keep to these rules, and one draw needn't show every extreme that they name: `low_rows`: 16 distinct block indices; the first and the last ancestor block are always among them. `sigma_anc`: symmetric. `top_dinv`: symmetric. `low_dinv`: symmetric.
All inputs are finite; a program needn't handle non-finite values.
Results may differ from the reference program's by a relative error of at most 0.0085.
Values may be sent and summed in bfloat16 or wider, within the bound.
No kernel may reach another device: no remote copies, remote signals or barrier semaphores. Data moves between devices by JAX's collectives and lax.ppermute only.
A program may use at most 128 MiB of HBM per device.

```python
import jax
import jax.numpy as jnp

BLOCK = 128
W = 4096
SA = 4096
LOW_BLOCKS = 16
NBLK = 32


def symmetric_block(key, salt, order, spread, low_diag, high_diag):
    seeded = jax.random.fold_in(key, salt)
    first, second = jax.random.split(seeded, 2)
    normal_part = jax.random.normal(first, (order, order), jnp.float32)
    diagonal = jax.random.uniform(second, (order,), jnp.float32, low_diag, high_diag)
    identity = (jnp.arange(order)[:, None] == jnp.arange(order)[None, :]).astype(jnp.float32)
    matrix = (normal_part + normal_part.T) * (0.7071 * spread) + identity * diagonal[None, :]
    return matrix


def draw_sigma_anc(key, part):
    return symmetric_block(key, 10, SA, 1.0, 1.0, 3.0).astype(jnp.bfloat16)


def draw_top_dinv(key, part):
    return symmetric_block(key, 11, W, 0.3, 1.0, 3.0).astype(jnp.bfloat16)


def draw_low_dinv(key, part):
    return symmetric_block(key, 12, W, 0.3, 1.0, 3.0).astype(jnp.bfloat16)


def draw_low_rows(key, part):
    seeded = jax.random.fold_in(key, 13)
    inner = jax.random.permutation(seeded, NBLK - 2)[:LOW_BLOCKS - 2].astype(jnp.int32) + 1
    first_block = jnp.zeros((1,), jnp.int32)
    last_block = jnp.full((1,), NBLK - 1, jnp.int32)
    return jnp.concatenate([first_block, inner, last_block])


def block_scale(key, extent, pieces, smallest, high):
    loudness = 1.0
    for dim, shards_of in pieces:
        steps = jax.random.uniform(jax.random.fold_in(jax.random.fold_in(key, 6), dim), (shards_of,), jnp.float32, smallest / len(pieces), high / len(pieces))
        loudness = loudness * jnp.repeat(jnp.exp(steps), extent[dim] // shards_of).reshape((-1,) + (1,) * (len(extent) - 1 - dim))
    return loudness


def gaussian(stream_key, shape, deviation, bound, cuts=(), held_as=jnp.bfloat16):
    drawn = deviation * jax.random.normal(stream_key, shape, jnp.float32)
    if cuts:
        drawn = drawn * block_scale(stream_key, shape, cuts, -0.22, 0.18)
    return jnp.clip(drawn, -bound, bound).astype(held_as)


def setup_inputs(seed: int = 0) -> dict:
    arg_keys = jax.random.split(jax.random.key(seed), 8)
    sigma_anc = draw_sigma_anc(jax.random.fold_in(arg_keys[7], 71), 0)
    top_panel = gaussian(arg_keys[1], (SA, W), SA ** -0.5, 0.09375, ((0, 2), (1, 16)))
    top_dinv = draw_top_dinv(jax.random.fold_in(arg_keys[7], 71), 0)
    low_upper = gaussian(arg_keys[3], (W, W), W ** -0.5, 0.09375, ((0, 2), (1, 16)))
    low_ancestor = gaussian(arg_keys[4], (SA, W), SA ** -0.5, 0.09375, ((0, 2), (1, 16)))
    low_dinv = draw_low_dinv(jax.random.fold_in(arg_keys[7], 71), 0)
    low_rows = draw_low_rows(jax.random.fold_in(arg_keys[7], 71), 0)
    return dict(sigma_anc=sigma_anc, top_panel=top_panel, top_dinv=top_dinv, low_upper=low_upper, low_ancestor=low_ancestor, low_dinv=low_dinv, low_rows=low_rows)


def reference(sigma_anc, top_panel, top_dinv, low_upper, low_ancestor, low_dinv, low_rows):
    row_ids = jnp.arange(SA, dtype=jnp.int32) // BLOCK
    in_pattern = jnp.any(row_ids[:, None] == low_rows[None, :], axis=1).astype(jnp.float32)[:, None]
    masked = (low_ancestor.astype(jnp.float32) * in_pattern).astype(jnp.bfloat16)
    top_off = (-jnp.dot(sigma_anc, top_panel, preferred_element_type=jnp.float32)).astype(jnp.bfloat16)
    top_diag = (top_dinv.astype(jnp.float32) - jnp.dot(top_off.T, top_panel, preferred_element_type=jnp.float32)).astype(jnp.bfloat16)
    cross = jnp.dot(top_off.T, masked, preferred_element_type=jnp.float32)
    ancestor_sum = jnp.dot(top_off, low_upper, preferred_element_type=jnp.float32) + jnp.dot(sigma_anc, masked, preferred_element_type=jnp.float32)
    low_anc = (-in_pattern * ancestor_sum).astype(jnp.bfloat16)
    low_top = (-(jnp.dot(top_diag, low_upper, preferred_element_type=jnp.float32) + cross)).astype(jnp.bfloat16)
    low_terms = jnp.dot(low_top.T, low_upper, preferred_element_type=jnp.float32) + jnp.dot(low_anc.T, masked, preferred_element_type=jnp.float32)
    low_diag = (low_dinv.astype(jnp.float32) - low_terms).astype(jnp.bfloat16)
    return (top_off, top_diag, low_top, low_anc, low_diag)
```

```python
import jax
import jax.numpy as jnp
from jax import lax
from jax.sharding import PartitionSpec as P

BLOCK = 128
F32 = jnp.float32
BF16 = jnp.bfloat16


def solution(mesh):
    R, C = mesh.shape["row"], mesh.shape["col"]
    n = C // 2
    hb = n // R
    order = list(range(0, n, 2)) + list(range(n - 1, 0, -2))
    place = [order.index(c) for c in range(n)]

    def ring_perm(shift):
        return [
            (c * 2 + k, order[(place[c] + shift) % n] * 2 + k) for c in range(n) for k in range(2)
        ]

    ring_perms = {1: ring_perm(1), -1: ring_perm(-1)}
    core_perm = [(i, i ^ 1) for i in range(C)]

    def core_swap(x):
        return lax.ppermute(x, "col", core_perm)

    def row_swap(x):
        return lax.ppermute(x, "row", [(0, 1), (1, 0)])

    def body(sigma, top_panel, top_dinv, low_upper, low_ancestor, low_dinv, low_rows):
        rows, w = sigma.shape
        r = lax.axis_index("row")
        col = lax.axis_index("col")
        c, k = col // 2, col % 2
        pos = jnp.asarray(place, jnp.int32)[c]

        def origin(shift):
            return jnp.asarray(order, jnp.int32)[(pos - shift + n) % n]

        def slot(chip):
            if R == 2:
                return ((chip // hb) ^ r) * hb + chip % hb
            return chip

        def ring_steps(x, forward, back):
            chunks = [(0, x)]
            a = b = x
            for s in range(1, max(forward, back) + 1):
                if s <= forward:
                    a = lax.ppermute(a, "col", ring_perms[1])
                    chunks.append((s, a))
                if s <= back:
                    b = lax.ppermute(b, "col", ring_perms[-1])
                    chunks.append((-s, b))
            return chunks, (a, b)

        lanes = []

        def ring(x, wide):
            if lanes:
                x, _ = lax.optimization_barrier((x, lanes[-1]))
            long, short = n // 2, n - 1 - n // 2
            chunks, last = ring_steps(x, *((long, short) if wide else (short, long)))
            lanes.append(last)
            return chunks

        def from_core(mine, theirs):
            first = jnp.where(k == 0, mine, theirs)
            second = jnp.where(k == 0, theirs, mine)
            return jnp.stack([first, second], axis=1).reshape(rows, mine.shape[-1])

        def core_columns(x):
            return jnp.concatenate([x, core_swap(x)], axis=-1)

        def panel(x):
            x4 = x.reshape(hb, 2, w, w)
            keep = lax.dynamic_index_in_dim(x4, k, 1, keepdims=False)
            send = lax.dynamic_index_in_dim(x4, 1 - k, 1, keepdims=False)
            here = jnp.concatenate([keep, core_swap(send)], axis=-1)
            if R == 2:
                return jnp.concatenate([here, row_swap(here)], axis=0)
            return lax.all_gather(here, "row", axis=0, tiled=True)

        def times(chunks, right):
            total = 0.0
            for shift, chunk in chunks:
                block = lax.dynamic_index_in_dim(right, slot(origin(shift)), 0, keepdims=False)
                total = total + jnp.dot(chunk, block, preferred_element_type=F32)
            return total[:, :w] + core_swap(total[:, w:].astype(BF16)).astype(F32)

        def times_t(pairs):
            out = jnp.zeros((n, w, 2 * w), BF16)
            for i in range(n):
                part = 0.0
                for chunks, right in pairs:
                    shift, chunk = chunks[i]
                    part = part + lax.dot_general(
                        chunk, right, (((0,), (0,)), ((), ())), preferred_element_type=F32
                    )
                out = lax.dynamic_update_index_in_dim(
                    out, part.astype(BF16), slot(origin(shift)), 0
                )
            if R == 2:
                return out[:hb].astype(F32) + row_swap(out[hb:]).astype(F32)
            return lax.psum_scatter(out, "row", scatter_dimension=0, tiled=True).astype(F32)

        row_ids = (r * rows + jnp.arange(rows, dtype=jnp.int32)) // BLOCK
        in_pattern = jnp.any(row_ids[:, None] == low_rows[None, :], axis=1)[:, None]
        masked = jnp.where(in_pattern, low_ancestor, jnp.zeros_like(low_ancestor))

        share = low_rows.shape[0] // R
        blocks = lax.dynamic_slice_in_dim(low_rows, r * share, share)

        def pack(x):
            if R == 2:
                both = jnp.concatenate([x, row_swap(x)], axis=0)
                rank = lambda b: ((b // (rows // BLOCK)) ^ r) * (rows // BLOCK) + b % (rows // BLOCK)
            else:
                both = lax.all_gather(x, "row", axis=0, tiled=True)
                rank = lambda b: b
            return jnp.concatenate(
                [
                    lax.dynamic_slice_in_dim(both, rank(blocks[i]) * BLOCK, BLOCK, 0)
                    for i in range(share)
                ],
                axis=0,
            )

        top_ring = ring(top_panel, True)
        upper_panel = panel(low_upper)
        sigma_ring = ring(sigma, False)
        top_right = panel(top_panel)
        dinv_ring = ring(top_dinv, True)
        packed = pack(low_ancestor)
        packed_ring = ring(packed, False)
        upper_ring = ring(low_upper, True)

        v = (masked.astype(F32) - times(top_ring, upper_panel)).astype(BF16)
        top_off = (-times(sigma_ring, top_right)).astype(BF16)
        x = (-times(sigma_ring, panel(v))).astype(BF16)
        low_anc = jnp.where(in_pattern, x, jnp.zeros_like(x))
        x_packed = core_columns(pack(x))

        def own_columns(y):
            return from_core(y[..., :w], core_swap(y[..., w:]))

        top_diag = (
            top_dinv.astype(F32) - own_columns(times_t([(top_ring, core_columns(top_off))]))
        ).astype(BF16)
        by_shift = lambda chunks: sorted(chunks, key=lambda item: item[0] % n)
        top_s, dinv_s, upper_s, packed_s = map(
            by_shift, (top_ring, dinv_ring, upper_ring, packed_ring)
        )
        low_top_k = (
            -times_t([(dinv_s, core_columns(low_upper)), (top_s, core_columns(x))])
        ).astype(BF16)
        other = core_swap(low_top_k)
        low_top_both = from_core(
            low_top_k, jnp.concatenate([other[..., w:], other[..., :w]], axis=-1)
        )
        low_top = low_top_both[:, :w]
        low_diag = (
            low_dinv.astype(F32)
            - own_columns(times_t([(packed_s, x_packed), (upper_s, low_top_both)]))
        ).astype(BF16)
        return (top_off, top_diag, low_top, low_anc, low_diag)

    spec = P("row", "col")
    return jax.shard_map(
        body, mesh=mesh, in_specs=(spec,) * 6 + (P(),), out_specs=(spec,) * 5, check_vma=False
    )
```

```python
import jax
import jax.numpy as jnp
import numpy as np
from jax import lax
from jax.experimental import pallas as pl
from jax.experimental.pallas import tpu as pltpu
from jax.sharding import PartitionSpec as P

BLOCK = 128
F32 = jnp.float32
BF16 = jnp.bfloat16
VMEM_BYTES = 56 * 1024 * 1024


def dot(a, b):
    return jnp.dot(a, b, preferred_element_type=F32)


def dot_t(a, b):
    return lax.dot_general(a, b, (((0,), (0,)), ((), ())), preferred_element_type=F32)


def cost(flops=0, bytes_accessed=0):
    return pl.CostEstimate(flops=1, bytes_accessed=1, transcendentals=0)


def params():
    return pltpu.CompilerParams(vmem_limit_bytes=VMEM_BYTES)


def at(index, size):
    return pl.ds(pl.multiple_of(index * size, size), size)


def whole(x):
    return pl.BlockSpec(x.shape, lambda i, idx: (0, 0))


def copy_block(out, place, panel, index, w):
    per = panel[0].shape[0] // w
    for j in range(0, len(panel), 2):

        @pl.when(index // per == j // 2)
        def _():
            rows = at(index - (j // 2) * per, w)
            out[pl.ds(place * w, w), :w] = panel[j][rows, :]
            out[pl.ds(place * w, w), w:] = panel[j + 1][rows, :]


def take_blocks(parts, idx, size):
    count, width = idx.shape[0], parts[0].shape[1]
    m = len(parts)
    per = parts[0].shape[0] // size

    def kernel(idx_ref, *refs):
        o = refs[m]
        if m == 1:
            o[...] = refs[0][...]
        for j in range(m if m > 1 else 0):

            @pl.when(idx_ref[pl.program_id(0)] // per == j)
            def _():
                o[...] = refs[j][...]

    return pl.pallas_call(
        kernel,
        grid_spec=pltpu.PrefetchScalarGridSpec(
            num_scalar_prefetch=1,
            grid=(count,),
            in_specs=[pl.BlockSpec((size, width), lambda i, idx: (idx[i] % per, 0))] * m,
            out_specs=pl.BlockSpec((size, width), lambda i, idx: (i, 0)),
        ),
        out_shape=jax.ShapeDtypeStruct((count * size, width), parts[0].dtype),
        cost_estimate=cost(0, 4 * count * size * width),
    )(idx, *parts)


def times(chunks, panel, idx):
    m = len(chunks)
    counts = [len(pieces) for pieces in chunks]
    rows, w = sum(x.shape[0] for x in chunks[0]), chunks[0][0].shape[1]
    tile = min(256, rows // 2)
    steps = rows // tile

    def kernel(idx_ref, *refs):
        own, send, right = refs[-3:]
        pieces, rest = split(refs[:-3], counts)
        step = pl.program_id(0)

        @pl.when(step == 0)
        def _():
            for s in range(m):
                copy_block(right, s, rest, idx_ref[s], w)

        def block(refs):
            value = refs[0][...]
            for i in range(1, len(refs)):
                value = jnp.where(step // (steps // len(refs)) == i, refs[i][...], value)
            return value

        total = dot(jnp.concatenate([block(x) for x in pieces], axis=1), right[...])
        own[...] = total[:, :w]
        send[...] = total[:, w:].astype(BF16)

    def piece(part, count):
        each = steps // count
        return pl.BlockSpec((tile, w), lambda i, idx: (jnp.clip(i - part * each, 0, each - 1), 0))

    return pl.pallas_call(
        kernel,
        grid_spec=pltpu.PrefetchScalarGridSpec(
            num_scalar_prefetch=1,
            grid=(steps,),
            in_specs=[piece(part, count) for count in counts for part in range(count)]
            + [whole(x) for x in panel],
            out_specs=[pl.BlockSpec((tile, w), lambda i, idx: (i, 0))] * 2,
            scratch_shapes=[pltpu.VMEM((m * w, 2 * w), BF16)],
        ),
        out_shape=[
            jax.ShapeDtypeStruct((rows, w), F32),
            jax.ShapeDtypeStruct((rows, w), BF16),
        ],
        compiler_params=params(),
        cost_estimate=cost(),
    )(idx, *sum(chunks, []), *panel)


def load_all(chunks, held, sems):
    waits = []
    for s, pieces in enumerate(chunks):
        base, copies = 0, []
        for i, piece in enumerate(pieces):
            size = piece.shape[0]
            copies.append(
                pltpu.make_async_copy(piece, held.at[s, pl.ds(base, size)], sems.at[s, i])
            )
            copies[-1].start()
            base += size
        waits.append(copies)

    def wait(s):
        for copy in waits[s]:
            copy.wait()

    return wait


def split(refs, counts):
    out, base = [], 0
    for count in counts:
        out.append(list(refs[base : base + count]))
        base += count
    return out, refs[base:]


def times_t(chunks, right, idx, form, start=()):
    m = len(chunks)
    counts = [len(pieces) for pieces in chunks]
    rows, w = sum(x.shape[0] for x in chunks[0]), chunks[0][0].shape[1]
    ANY = pl.BlockSpec(memory_space=pl.ANY)
    kept = lambda shape, dtype: jax.ShapeDtypeStruct(shape, dtype)
    if form == "blocks":
        outs = [kept((m * w, 2 * w), BF16)]
    elif form == "add":
        outs = [kept(x.shape, x.dtype) for x in start]
    else:
        outs = [kept((m // 2 * w, 2 * w), t) for t in (F32, BF16)]

    def kernel(idx_ref, *refs):
        hbm, rest = split(refs, counts)
        right_refs, rest = rest[: len(right)], rest[len(right) :]
        start_refs, rest = rest[: len(start)], rest[len(start) :]
        out, (both, held, sems) = rest[: len(outs)], rest[len(outs) :]
        wait = load_all(hbm, held, sems)
        base = 0
        for j in range(0, len(right), 2):
            size = right[j].shape[0]
            both[base : base + size, :w] = right_refs[j][...]
            both[base : base + size, w:] = right_refs[j + 1][...]
            base += size
        for i in range(len(start)):
            out[i][...] = start_refs[i][...]
        for s in range(m):
            wait(s)
            value = dot_t(held[s], both[...])
            if form == "blocks":
                out[0][at(idx_ref[s], w), :] = value.astype(BF16)
            elif form == "add":
                place = at(idx_ref[s], w)
                out[0][place, :] = out[0][place, :] + value[:, :w]
                out[1][place, :] = (out[1][place, :].astype(F32) + value[:, w:]).astype(BF16)
            else:
                place = pl.ds(s // 2 * w, w)

                @pl.when(idx_ref[s] == 1)
                def _():
                    out[0][place, :] = value

                @pl.when(idx_ref[s] == 0)
                def _():
                    out[1][place, :] = value.astype(BF16)

    return pl.pallas_call(
        kernel,
        grid_spec=pltpu.PrefetchScalarGridSpec(
            num_scalar_prefetch=1,
            grid=(1,),
            in_specs=[ANY] * sum(counts) + [whole(x) for x in (*right, *start)],
            out_specs=[whole(x) for x in outs],
            scratch_shapes=[
                pltpu.VMEM((rows, 2 * w), BF16),
                pltpu.VMEM((m, rows, w), BF16),
                pltpu.SemaphoreType.DMA((m, max(counts))),
            ],
        ),
        out_shape=outs,
        compiler_params=params(),
        cost_estimate=cost(4 * m * rows * w * w, 0),
    )(idx, *sum(chunks, []), *right, *start)


def finish(base, parts, idx, k):
    rows, w = base.shape
    counts = [x[2].shape[0] // w for x in parts]

    def kernel(idx_ref, k_ref, base_ref, *refs):
        out = refs[-1]
        j = 0
        for i, count in enumerate(counts):
            mine, rest, other = refs[3 * i : 3 * i + 3]
            for b in range(count):
                block = slice(b * w, (b + 1) * w)
                for core, value in (
                    (k_ref[0], mine[block, :w] + rest[block, :w].astype(F32)),
                    (1 - k_ref[0], other[block, :]),
                ):
                    place = at(2 * idx_ref[j] + core, w)
                    out[place, :] = (base_ref[place, :].astype(F32) - value).astype(BF16)
                j += 1

    return pl.pallas_call(
        kernel,
        grid_spec=pltpu.PrefetchScalarGridSpec(
            num_scalar_prefetch=2,
            grid=(1,),
            in_specs=[
                pl.BlockSpec(x.shape, lambda i, idx, k: (0, 0)) for x in (base, *sum(parts, ()))
            ],
            out_specs=pl.BlockSpec(base.shape, lambda i, idx, k: (0, 0)),
        ),
        out_shape=jax.ShapeDtypeStruct(base.shape, BF16),
        compiler_params=params(),
        cost_estimate=cost(0, 8 * base.size),
    )(idx, k, base, *sum(parts, ()))


def times_symmetric(chunks, panel, table, slots):
    m = len(chunks)
    counts = [len(pieces) for pieces in chunks]
    w = chunks[0][0].shape[1]
    height = sum(x.shape[0] for x in panel) // 2
    inner = slots - 2
    ANY = pl.BlockSpec(memory_space=pl.ANY)

    def kernel(t, *refs):
        hbm, rest = split(refs, counts)
        panel_refs = rest[: len(panel)]
        own, send, acc, p, few, c, sems = rest[len(panel) :]
        wait = load_all(hbm, c, sems)
        base = 0
        for j in range(0, len(panel), 2):
            size = panel[j].shape[0]
            p[base : base + size, :w] = panel_refs[j][...]
            p[base : base + size, w:] = panel_refs[j + 1][...]
            base += size
        acc[...] = jnp.zeros_like(acc)

        def add(index, value):
            acc[at(index, w), :] = acc[at(index, w), :] + value

        for s in range(m):
            b0 = s * (slots + 3)
            q = t[b0]
            row = lambda b: t[b0 + 1 + b]
            wait(s)
            right_q = p[at(q, w), :]
            for b in range(1, slots - 1):
                few[(b - 1) * w : b * w, :] = p[at(row(b), w), :]
            part = dot(c[s, : (slots - 1) * w, :], right_q)
            for b in range(slots - 1):
                add(row(b), part[b * w : (b + 1) * w])
            add(q, dot_t(c[s, w : (slots - 1) * w, :], few[...]))

            @pl.when(t[b0 + 1 + slots] == 1)
            def _():
                add(q, dot_t(c[s, :w, :], p[at(row(0), w), :]))

            @pl.when(t[b0 + 2 + slots] == 1)
            def _():
                last = c[s, (slots - 1) * w :, :]
                add(row(slots - 1), dot(last, right_q))
                add(q, dot_t(last, p[at(row(slots - 1), w), :]))

        own[...] = acc[:, :w]
        send[...] = acc[:, w:].astype(BF16)

    return pl.pallas_call(
        kernel,
        grid_spec=pltpu.PrefetchScalarGridSpec(
            num_scalar_prefetch=1,
            grid=(1,),
            in_specs=[ANY] * sum(counts) + [whole(x) for x in panel],
            out_specs=[pl.BlockSpec((height, w), lambda i, t: (0, 0))] * 2,
            scratch_shapes=[
                pltpu.VMEM((height, 2 * w), F32),
                pltpu.VMEM((height, 2 * w), BF16),
                pltpu.VMEM((inner * w, 2 * w), BF16),
                pltpu.VMEM((m, slots * w, w), BF16),
                pltpu.SemaphoreType.DMA((m, max(counts))),
            ],
        ),
        out_shape=[
            jax.ShapeDtypeStruct((height, w), F32),
            jax.ShapeDtypeStruct((height, w), BF16),
        ],
        compiler_params=params(),
        cost_estimate=cost(2 * height * height * w, 0),
    )(table, *sum(chunks, []), *panel)


def solution(mesh):
    R, C = mesh.shape["row"], mesh.shape["col"]
    n = C // 2
    nb = C // R
    slots = nb // 2 + 1
    order = list(range(0, n, 2)) + list(range(n - 1, 0, -2))
    place = [order.index(c) for c in range(n)]
    shifts = list(range(n))
    pairs = [(s, s + n // 2) for s in range(n // 2)]

    def ring_perm(shift):
        return [
            (c * 2 + k, order[(place[c] + shift) % n] * 2 + k) for c in range(n) for k in range(2)
        ]

    ring_perms = {1: ring_perm(1), -1: ring_perm(-1)}
    core_perm = [(i, i ^ 1) for i in range(C)]

    def slot(x, q):
        return ((q // nb) ^ x) * nb + q % nb if R == 2 else q

    def provided(x, q):
        h, lq = q // nb, q % nb
        if h == x:
            return [(lq + b) % nb for b in range(slots)]
        return [(lq + 2 * b + (x > h)) % nb for b in range(slots - 1)] + [0]

    def rows_of(make):
        return np.array([[make(x, col) for col in range(C)] for x in range(R)], np.int32)

    def source(col, shift):
        return order[(place[col // 2] - shift) % n] * 2 + col % 2

    def symmetric_row(x, col):
        out = []
        for s in shifts:
            q = source(col, s)
            inside = q // nb == x
            out += [slot(x, q)] + [slot(x, x * nb + i) for i in provided(x, q)]
            out += [int(not inside), int(inside and q % nb < nb // 2)]
        return out

    def pair_row(x, col):
        mine = [int(source(col, s) // nb == x) for pair in pairs for s in pair]
        return mine + [
            source(col, s) % nb // 2 for pair in pairs for s in pair if source(col, s) // nb == x
        ]

    send_table = rows_of(provided)
    column_table = rows_of(lambda x, col: [slot(x, source(col, s)) for s in shifts])
    chip_table = rows_of(lambda x, col: [slot(x, source(col, s)) // 2 for s in shifts])
    symmetric_table = rows_of(symmetric_row)
    pair_table = rows_of(pair_row) if R == 2 else chip_table

    def core_swap(x):
        return lax.ppermute(x, "col", core_perm)

    def row_swap(x):
        return lax.ppermute(x, "row", [(0, 1), (1, 0)])

    def body(sigma, top_panel, top_dinv, low_upper, low_ancestor, low_dinv, low_rows):
        rows, w = sigma.shape
        r = lax.axis_index("row")
        col = lax.axis_index("col")
        k = col % 2
        here = lambda table: lax.dynamic_slice(
            jnp.asarray(table), (r, col, 0), (1, 1, table.shape[2])
        ).reshape(-1)
        column_idx, chip_idx, symmetric_idx, send_idx, pair_idx = map(
            here, (column_table, chip_table, symmetric_table, send_table, pair_table)
        )

        def gather_rows(x):
            if R == 2:
                return [x, row_swap(x)]
            return [lax.all_gather(x, "row", axis=0, tiled=True)]

        def both_cores(pieces):
            return [y for x in pieces for y in (x, core_swap(x))]

        def scatter_rows(x):
            if R == 2:
                half = x.shape[0] // 2
                return [x[:half], row_swap(x[half:].astype(BF16))]
            return [lax.psum_scatter(x.astype(BF16), "row", scatter_dimension=0, tiled=True)]

        def add(parts):
            return sum((x.astype(F32) for x in parts[1:]), parts[0].astype(F32))

        def own_columns(y):
            y = y.reshape(nb // 2, w, 2 * w)
            mine, theirs = y[..., :w], core_swap(y[..., w:])
            first = jnp.where(k == 0, mine, theirs)
            second = jnp.where(k == 0, theirs, mine)
            return jnp.stack([first, second], axis=1).reshape(rows, w)

        row_ids = (r * rows + jnp.arange(rows, dtype=jnp.int32)) // BLOCK
        in_pattern = jnp.any(row_ids[:, None] == low_rows[None, :], axis=1)[:, None]

        share = low_rows.shape[0] // R
        pattern_idx = lax.dynamic_slice_in_dim(low_rows, r * share, share)
        if R == 2:
            count = rows // BLOCK
            other_idx = lax.dynamic_slice_in_dim(low_rows, (1 - r) * share, share)
            pack_idx = jnp.concatenate([pattern_idx, other_idx]) % count
            pack_here = jnp.repeat(pattern_idx // count == r, BLOCK)[:, None]
        else:
            pack_idx = pattern_idx

        def take_pattern(x):
            return take_blocks([x], pack_idx, BLOCK) if R == 2 else x

        def pack_rows(taken):
            if R == 2:
                cut = share * BLOCK
                return [taken[:cut], row_swap(taken[cut:])]
            return [lax.all_gather(taken, "row", axis=0, tiled=True)]

        def packed(parts):
            if R == 2:
                return jnp.where(pack_here, *parts)
            return take_blocks(parts, pattern_idx, BLOCK)

        steps = n // 2
        stages = 4
        env, due, events = {}, {}, {}
        rings = [{} for _ in range(stages)]

        def step_of(stage, j):
            return stage * steps + (j * (steps - 1) + 2) // 3

        def on(stage, j):
            def register(f):
                events.setdefault(step_of(stage, j), []).append(f)

            return register

        def keep(name, value, *until):
            env[name] = value
            if until:
                due[name] = step_of(*until)

        def ring_of(stage):
            return [env["ring", stage, s] for s in shifts]

        def core_sum(parts):
            own, send = parts
            return own + core_swap(send).astype(F32)

        @on(0, 0)
        def _():
            keep("upper_rows", gather_rows(low_upper), 0, 1)
            env["sigma_send"] = take_blocks([sigma], send_idx, w)
            env["dinv_send"] = take_blocks([top_dinv], send_idx, w)
            env["low_taken"] = take_pattern(low_ancestor)

        @on(0, 1)
        def _():
            keep("low_parts", pack_rows(env["low_taken"]), 0, 1)

        @on(0, 2)
        def _():
            env["upper"] = both_cores(env["upper_rows"])
            keep("top_rows", gather_rows(top_panel), 0, 3)
            env["low_send"] = jnp.concatenate([low_upper, packed(env["low_parts"])], axis=0)

        @on(1, 0)
        def _():
            env["v_parts"] = times(ring_of(0), env["upper"], env["column_idx"])

        @on(1, 1)
        def _():
            masked = jnp.where(in_pattern, low_ancestor, jnp.zeros_like(low_ancestor))
            v = (masked.astype(F32) - core_sum(env.pop("v_parts"))).astype(BF16)
            keep("v_rows", gather_rows(v), 1, 2)

        @on(1, 2)
        def _():
            env["top_right"] = both_cores(env["top_rows"])

        @on(1, 3)
        def _():
            env["v_right"] = both_cores(env["v_rows"])

        @on(2, 0)
        def _():
            env["x_parts"] = times_symmetric(
                ring_of(1), env["v_right"], env["symmetric_idx"], slots
            )

        @on(2, 1)
        def _():
            keep("x_sum", scatter_rows(core_sum(env.pop("x_parts"))), 2, 2)

        @on(2, 2)
        def _():
            env["off_parts"] = times_symmetric(
                ring_of(1), env["top_right"], env["symmetric_idx"], slots
            )

        @on(2, 3)
        def _():
            x = (-add(env.pop("x_sum"))).astype(BF16)
            env["low_anc"] = jnp.where(in_pattern, x, jnp.zeros_like(x))
            env["x"] = both_cores([x])
            keep("off_sum", scatter_rows(core_sum(env.pop("off_parts"))), 3, 0)

        @on(3, 0)
        def _():
            dinv_upper = times_symmetric(
                ring_of(2), env["upper"], env["symmetric_idx"], slots
            )
            env["low_top_parts"] = times_t(
                ring_of(0), env["x"], env["column_idx"], "add", dinv_upper
            )

        @on(3, 1)
        def _():
            keep("low_top_sum", scatter_rows(core_sum(env.pop("low_top_parts"))), 3, 1)
            env["x_taken"] = take_pattern(env["x"][0])
            env["top_off"] = (-add(env.pop("off_sum"))).astype(BF16)
            env["diag_parts"] = times_t(
                ring_of(0), both_cores([env["top_off"]]), env["chip_idx"], "blocks"
            )[0]

        @on(3, 2)
        def _():
            env["low_top"] = (-add(env.pop("low_top_sum"))).astype(BF16)
            env["low_top_both"] = both_cores([env["low_top"]])
            env["x_packed"] = both_cores([packed(pack_rows(env["x_taken"]))])
            keep("diag_sum", scatter_rows(env.pop("diag_parts")), 3, 3)

        def diag_part(some):
            low_right = env["low_top_both"] + env["x_packed"]
            which = jnp.concatenate([env["pair_idx"][2 * j : 2 * j + 2] for j in some])
            chunks = [env["ring", 3, s] for j in some for s in pairs[j]]
            return times_t(chunks, low_right, which, "pairs")

        def diag_rest(mine, rest):
            rest = row_swap(rest)
            return mine, rest, core_swap(mine[:, w:] + rest[:, w:].astype(F32))

        if R == 2:

            @on(3, 3)
            def _():
                env["diag_first"] = diag_part(range(1, n // 2))

        env.update(
            column_idx=column_idx, chip_idx=chip_idx, symmetric_idx=symmetric_idx, pair_idx=pair_idx
        )

        def send(step):
            stage, hop = step // steps, step % steps + 1
            if hop == 1:
                name = ("top_send", "sigma_send", "dinv_send", "low_send")[stage]
                env["ring", stage, 0] = [top_panel if stage == 0 else env[name]]
            held = [env["ring", stage, way * (hop - 1) % n][0] for way in (1, -1)]
            if hop == steps:
                half = held[0].shape[0] // 2
                held = [held[0][:half], held[1][half:]]
            got = [lax.ppermute(x, "col", ring_perms[way]) for x, way in zip(held, (1, -1))]
            if hop == steps:
                return {("ring", stage, steps): got}
            return {("ring", stage, way * hop % n): [x] for x, way in zip(got, (1, -1))}

        for g in range(stages * steps):
            arriving = send(g)
            for event in events.get(g, []):
                event()
            env.update(arriving)
            names = [name for name in env if due.get(name, 0) <= g]
            leaves, tree = jax.tree.flatten([env[name] for name in names])
            env.update(zip(names, jax.tree.unflatten(tree, lax.optimization_barrier(leaves))))

        if R == 2:
            first = diag_rest(*env["diag_first"])
            parts = [first, diag_rest(*diag_part(range(1)))]
            places = jnp.concatenate([pair_idx[n + 1 :], pair_idx[n : n + 1]])
            low_diag = finish(low_dinv, parts, places, k.reshape(1))
        else:
            right = env["low_top_both"] + env["x_packed"]
            total = add(scatter_rows(times_t(ring_of(3), right, chip_idx, "blocks")[0]))
            low_diag = (low_dinv.astype(F32) - own_columns(total)).astype(BF16)
        top_diag = (top_dinv.astype(F32) - own_columns(add(env["diag_sum"]))).astype(BF16)
        return (env["top_off"], top_diag, env["low_top"], env["low_anc"], low_diag)

    spec = P("row", "col")
    return jax.shard_map(
        body, mesh=mesh, in_specs=(spec,) * 6 + (P(),), out_specs=(spec,) * 5, check_vma=False
    )
```

```python
import jax
import jax.numpy as jnp
import numpy as np
from jax import lax
from jax.experimental import pallas as pl
from jax.experimental.pallas import tpu as pltpu
from jax.sharding import PartitionSpec as P

BLOCK = 128
F32 = jnp.float32
BF16 = jnp.bfloat16
VMEM_BYTES = 56 * 1024 * 1024


def dot(a, b):
    return jnp.dot(a, b, preferred_element_type=F32)


def dot_t(a, b):
    return lax.dot_general(a, b, (((0,), (0,)), ((), ())), preferred_element_type=F32)


def cost(flops=0, bytes_accessed=0):
    return pl.CostEstimate(flops=1, bytes_accessed=1, transcendentals=0)


def params():
    return pltpu.CompilerParams(vmem_limit_bytes=VMEM_BYTES)


def at(index, size):
    return pl.ds(pl.multiple_of(index * size, size), size)


def whole(x):
    return pl.BlockSpec(x.shape, lambda i, idx: (0, 0))


def copy_block(out, place, panel, index, w):
    per = panel[0].shape[0] // w
    for j in range(0, len(panel), 2):

        @pl.when(index // per == j // 2)
        def _():
            rows = at(index - (j // 2) * per, w)
            out[pl.ds(place * w, w), :w] = panel[j][rows, :]
            out[pl.ds(place * w, w), w:] = panel[j + 1][rows, :]


def take_symmetric(x, idx, base, slots):
    w = x.shape[1]
    half = w // 2

    def kernel(idx_ref, x_ref, o_ref):
        for b in range(slots - 1):
            o_ref[b * w : (b + 1) * w, :] = x_ref[at(idx_ref[base + b], w), :]
        block = x_ref[at(idx_ref[base + slots - 1], w), :]
        turned = idx_ref[base + slots] == 1

        @pl.when(turned)
        def _():
            o_ref[(slots - 1) * w :, :] = block[:, half:].T

        @pl.when(jnp.logical_not(turned))
        def _():
            o_ref[(slots - 1) * w :, :] = block[:half, :]

    return pl.pallas_call(
        kernel,
        grid_spec=pltpu.PrefetchScalarGridSpec(
            num_scalar_prefetch=1,
            grid=(1,),
            in_specs=[whole(x)],
            out_specs=pl.BlockSpec(((slots - 1) * w + half, w), lambda i, idx: (0, 0)),
        ),
        out_shape=jax.ShapeDtypeStruct(((slots - 1) * w + half, w), x.dtype),
        cost_estimate=cost(),
    )(idx, x)


def take_blocks(parts, idx, size, base=0, count=None):
    count, width = count or idx.shape[0], parts[0].shape[1]
    m = len(parts)
    per = parts[0].shape[0] // size

    def kernel(idx_ref, *refs):
        o = refs[m]
        if m == 1:
            o[...] = refs[0][...]
        for j in range(m if m > 1 else 0):

            @pl.when(idx_ref[base + pl.program_id(0)] // per == j)
            def _():
                o[...] = refs[j][...]

    return pl.pallas_call(
        kernel,
        grid_spec=pltpu.PrefetchScalarGridSpec(
            num_scalar_prefetch=1,
            grid=(count,),
            in_specs=[pl.BlockSpec((size, width), lambda i, idx: (idx[base + i] % per, 0))] * m,
            out_specs=pl.BlockSpec((size, width), lambda i, idx: (i, 0)),
        ),
        out_shape=jax.ShapeDtypeStruct((count * size, width), parts[0].dtype),
        cost_estimate=cost(0, 4 * count * size * width),
    )(idx, *parts)


def times(chunks, panel, idx, base):
    m = len(chunks)
    counts = [len(pieces) for pieces in chunks]
    rows, w = sum(x.shape[0] for x in chunks[0]), chunks[0][0].shape[1]
    tile = min(256, rows // 2)
    steps = rows // tile

    def kernel(idx_ref, *refs):
        own, send, right = refs[-3:]
        pieces, rest = split(refs[:-3], counts)
        step = pl.program_id(0)

        @pl.when(step == 0)
        def _():
            for s in range(m):
                copy_block(right, s, rest, idx_ref[base + s], w)

        def block(refs):
            value = refs[0][...]
            for i in range(1, len(refs)):
                value = jnp.where(step // (steps // len(refs)) == i, refs[i][...], value)
            return value

        total = dot(jnp.concatenate([block(x) for x in pieces], axis=1), right[...])
        own[...] = total[:, :w]
        send[...] = total[:, w:].astype(BF16)

    def piece(part, count):
        each = steps // count
        return pl.BlockSpec((tile, w), lambda i, idx: (jnp.clip(i - part * each, 0, each - 1), 0))

    return pl.pallas_call(
        kernel,
        grid_spec=pltpu.PrefetchScalarGridSpec(
            num_scalar_prefetch=1,
            grid=(steps,),
            in_specs=[piece(part, count) for count in counts for part in range(count)]
            + [whole(x) for x in panel],
            out_specs=[pl.BlockSpec((tile, w), lambda i, idx: (i, 0))] * 2,
            scratch_shapes=[pltpu.VMEM((m * w, 2 * w), BF16)],
        ),
        out_shape=[
            jax.ShapeDtypeStruct((rows, w), F32),
            jax.ShapeDtypeStruct((rows, w), BF16),
        ],
        compiler_params=params(),
        cost_estimate=cost(),
    )(idx, *sum(chunks, []), *panel)


def load_all(chunks, held, sems):
    waits = []
    for s, pieces in enumerate(chunks):
        base, copies = 0, []
        for i, piece in enumerate(pieces):
            size = piece.shape[0]
            copies.append(
                pltpu.make_async_copy(piece, held.at[s, pl.ds(base, size)], sems.at[s, i])
            )
            copies[-1].start()
            base += size
        waits.append(copies)

    def wait(s):
        for copy in waits[s]:
            copy.wait()

    return wait


def split(refs, counts):
    out, base = [], 0
    for count in counts:
        out.append(list(refs[base : base + count]))
        base += count
    return out, refs[base:]


def times_t(chunks, right, idx, at0, form, start=(), hand_on=False):
    m = len(chunks)
    counts = [len(pieces) for pieces in chunks]
    rows, w = sum(x.shape[0] for x in chunks[0]), chunks[0][0].shape[1]
    ANY = pl.BlockSpec(memory_space=pl.ANY)
    kept = lambda shape, dtype: jax.ShapeDtypeStruct(shape, dtype)
    if form == "blocks":
        outs = [kept((m * w, 2 * w), BF16)]
    elif form == "add":
        outs = [kept(x.shape, x.dtype) for x in start]
    else:
        outs = [kept(((m + 1) // 2 * w, w), t) for t in (F32, F32, BF16, BF16)]
    if hand_on:
        outs.append(kept((rows, 2 * w), BF16))

    def kernel(idx_ref, *refs):
        hbm, rest = split(refs, counts)
        right_refs, rest = rest[: len(right)], rest[len(right) :]
        start_refs, rest = rest[: len(start)], rest[len(start) :]
        out, (both, held, sems) = rest[: len(outs)], rest[len(outs) :]
        wait = load_all(hbm, held, sems)
        base = 0
        if len(right) == 1:
            both = right_refs[0]
        for j in range(0, len(right) - 1, 2):
            size = right[j].shape[0]
            both[base : base + size, :w] = right_refs[j][...]
            both[base : base + size, w:] = right_refs[j + 1][...]
            base += size
        for i in range(len(start)):
            out[i][...] = start_refs[i][...]
        if hand_on:
            out[-1][...] = both[...]
        for s in range(m):
            wait(s)
            value = dot_t(held[s], both[...])
            if form == "blocks":
                out[0][at(idx_ref[at0[s]], w), :] = value.astype(BF16)
            elif form == "add":
                place = at(idx_ref[at0[s]], w)
                out[0][place, :] = out[0][place, :] + value[:, :w]
                out[1][place, :] = (out[1][place, :].astype(F32) + value[:, w:]).astype(BF16)
            else:
                place = pl.ds(s // 2 * w, w)

                @pl.when(idx_ref[at0[s]] == 1)
                def _():
                    out[0][place, :] = value[:, :w]
                    out[1][place, :] = value[:, w:]

                @pl.when(idx_ref[at0[s]] == 0)
                def _():
                    out[2][place, :] = value[:, :w].astype(BF16)
                    out[3][place, :] = value[:, w:].astype(BF16)

    return pl.pallas_call(
        kernel,
        grid_spec=pltpu.PrefetchScalarGridSpec(
            num_scalar_prefetch=1,
            grid=(1,),
            in_specs=[ANY] * sum(counts) + [whole(x) for x in (*right, *start)],
            out_specs=[whole(x) for x in outs],
            scratch_shapes=[
                pltpu.VMEM((rows if len(right) > 1 else 16, 2 * w), BF16),
                pltpu.VMEM((m, rows, w), BF16),
                pltpu.SemaphoreType.DMA((m, max(counts))),
            ],
        ),
        out_shape=outs,
        compiler_params=params(),
        cost_estimate=cost(4 * m * rows * w * w, 0),
    )(idx, *sum(chunks, []), *right, *start)


def finish(base, own, other, idx, core, places, so_far=None):
    w = base.shape[1]
    count = own[0].shape[0] // w

    def kernel(idx_ref, base_ref, a, b, c, d, *rest):
        k = idx_ref[core]
        for place, x, y in ((at(k, w), a, b), (at(1 - k, w), c, d)):
            value = x[...].astype(F32) + y[...].astype(F32)
            rest[-1][place, :] = (base_ref[place, :].astype(F32) - value).astype(BF16)

    here = pl.BlockSpec((2 * w, w), lambda t, idx: (idx[places + t], 0))
    extra = [] if so_far is None else [so_far]
    return pl.pallas_call(
        kernel,
        grid_spec=pltpu.PrefetchScalarGridSpec(
            num_scalar_prefetch=1,
            grid=(count,),
            in_specs=[here]
            + [pl.BlockSpec((w, w), lambda t, idx: (t, 0))] * 4
            + [pl.BlockSpec(memory_space=pl.ANY) for _ in extra],
            out_specs=here,
        ),
        out_shape=jax.ShapeDtypeStruct(base.shape, BF16),
        input_output_aliases={} if so_far is None else {6: 0},
        cost_estimate=cost(),
    )(idx, base, *own, *other, *extra)


def times_symmetric(chunks, panel, table, base0, slots):
    m = len(chunks)
    counts = [len(pieces) for pieces in chunks]
    w = chunks[0][0].shape[1]
    height = sum(x.shape[0] for x in panel) // 2
    inner = slots - 2
    half = w // 2
    ANY = pl.BlockSpec(memory_space=pl.ANY)

    def kernel(t, *refs):
        hbm, rest = split(refs, counts)
        panel_refs = rest[: len(panel)]
        own, send, acc, p, few, c, sems = rest[len(panel) :]
        wait = load_all(hbm, c, sems)
        base = 0
        for j in range(0, len(panel), 2):
            size = panel[j].shape[0]
            p[base : base + size, :w] = panel_refs[j][...]
            p[base : base + size, w:] = panel_refs[j + 1][...]
            base += size
        acc[...] = jnp.zeros_like(acc)

        def add(index, value):
            acc[at(index, w), :] = acc[at(index, w), :] + value

        for s in range(m):
            b0 = base0 + s * (slots + 5)
            q = t[b0]
            row = lambda b: t[b0 + 1 + b]
            wait(s)
            right_q = p[at(q, w), :]
            for b in range(1, slots - 1):
                few[(b - 1) * w : b * w, :] = p[at(row(b), w), :]
            part = dot(c[s, : (slots - 1) * w, :], right_q)
            for b in range(slots - 1):
                add(row(b), part[b * w : (b + 1) * w])
            add(q, dot_t(c[s, w : (slots - 1) * w, :], few[...]))

            @pl.when(t[b0 + 3 + slots] == 1)
            def _():
                add(q, dot_t(c[s, :w, :], p[at(row(0), w), :]))

            @pl.when(t[b0 + 4 + slots] == 1)
            def _():
                last = c[s, (slots - 1) * w :, :]
                column = t[b0 + 1 + slots]
                place = at(2 * row(slots - 1) + t[b0 + 2 + slots], half)
                acc[place, :] = acc[place, :] + dot(last, p[at(column, w), :])
                add(column, dot_t(last, p[place, :]))

        own[...] = acc[:, :w]
        send[...] = acc[:, w:].astype(BF16)

    return pl.pallas_call(
        kernel,
        grid_spec=pltpu.PrefetchScalarGridSpec(
            num_scalar_prefetch=1,
            grid=(1,),
            in_specs=[ANY] * sum(counts) + [whole(x) for x in panel],
            out_specs=[pl.BlockSpec((height, w), lambda i, t: (0, 0))] * 2,
            scratch_shapes=[
                pltpu.VMEM((height, 2 * w), F32),
                pltpu.VMEM((height, 2 * w), BF16),
                pltpu.VMEM((inner * w, 2 * w), BF16),
                pltpu.VMEM((m, (slots - 1) * w + half, w), BF16),
                pltpu.SemaphoreType.DMA((m, max(counts))),
            ],
        ),
        out_shape=[
            jax.ShapeDtypeStruct((height, w), F32),
            jax.ShapeDtypeStruct((height, w), BF16),
        ],
        compiler_params=params(),
        cost_estimate=cost(2 * height * height * w, 0),
    )(table, *sum(chunks, []), *panel)


def solution(mesh):
    R, C = mesh.shape["row"], mesh.shape["col"]
    n = C // 2
    nb = C // R
    slots = nb // 2 + 1
    order = list(range(0, n, 2)) + list(range(n - 1, 0, -2))
    place = [order.index(c) for c in range(n)]
    shifts = list(range(n))
    pairs = [(s, s + n // 2) for s in range(n // 2)]

    def ring_perm(shift):
        return [
            (c * 2 + k, order[(place[c] + shift) % n] * 2 + k) for c in range(n) for k in range(2)
        ]

    ring_perms = {1: ring_perm(1), -1: ring_perm(-1)}
    core_perm = [(i, i ^ 1) for i in range(C)]

    def slot(x, q):
        return ((q // nb) ^ x) * nb + q % nb if R == 2 else q

    def provided(x, q):
        h, lq = q // nb, q % nb
        if h == x:
            return [(lq + b) % nb for b in range(slots - 1)]
        return [(lq + 2 * b + (x > h)) % nb for b in range(slots - 1)]

    def sent(x, q):
        return provided(x, q) + [(q + nb // 2) % nb, int(q % nb >= nb // 2)]

    def rows_of(make):
        return np.array([[make(x, col) for col in range(C)] for x in range(R)], np.int32)

    def source(col, shift):
        return order[(place[col // 2] - shift) % n] * 2 + col % 2

    def symmetric_row(x, col):
        out = []
        for s in shifts:
            q = source(col, s)
            inside = q // nb == x
            out += [slot(x, q)] + [slot(x, x * nb + i) for i in provided(x, q)]
            low = q % nb % (nb // 2)
            out += [slot(x, x * nb + low + nb // 2), slot(x, x * nb + low)]
            out += [int(q % nb >= nb // 2), int(not inside), int(inside)]
        return out

    near, far = list(range(2, n // 2 - 1)), [1, n // 2 - 1]
    table_of = dict(
        send=sent,
        column=lambda x, col: [slot(x, source(col, s)) for s in shifts],
        chip=lambda x, col: [slot(x, source(col, s)) // 2 for s in shifts],
        symmetric=symmetric_row,
        mine=lambda x, col: [int(source(col, s) // nb == x) for s in shifts],
        places=lambda x, col: [
            max(source(col, s) % nb // 2 * int(source(col, s) // nb == x) for s in pairs[j])
            for j in near + far + [0]
        ],
        core=lambda x, col: [col % 2],
    )
    offsets, table = {}, []
    for name, make in table_of.items():
        rows = rows_of(make)
        offsets[name] = sum(x.shape[2] for x in table)
        table.append(rows)
    table = np.concatenate(table, axis=2)

    def core_swap(x):
        return lax.ppermute(x, "col", core_perm)

    def row_swap(x):
        return lax.ppermute(x, "row", [(0, 1), (1, 0)])

    def both_swap(x):
        pairs = [(x * C + i, (1 - x) * C + (i ^ 1)) for x in range(2) for i in range(C)]
        return lax.ppermute(x, ("row", "col"), pairs)

    def body(sigma, top_panel, top_dinv, low_upper, low_ancestor, low_dinv, low_rows):
        rows, w = sigma.shape
        r = lax.axis_index("row")
        col = lax.axis_index("col")
        k = col % 2
        index = lax.dynamic_slice(
            jnp.asarray(table), (r, col, 0), (1, 1, table.shape[2])
        ).reshape(-1)

        def gather_rows(x):
            if R == 2:
                return [x, row_swap(x)]
            return [lax.all_gather(x, "row", axis=0, tiled=True)]

        def both_cores(pieces):
            return [y for x in pieces for y in (x, core_swap(x))]

        def scatter_rows(x):
            if R == 2:
                half = x.shape[0] // 2
                return [x[:half], row_swap(x[half:].astype(BF16))]
            return [lax.psum_scatter(x.astype(BF16), "row", scatter_dimension=0, tiled=True)]

        def add(parts):
            return sum((x.astype(F32) for x in parts[1:]), parts[0].astype(F32))

        def own_columns(y):
            y = y.reshape(nb // 2, w, 2 * w)
            mine, theirs = y[..., :w], core_swap(y[..., w:])
            first = jnp.where(k == 0, mine, theirs)
            second = jnp.where(k == 0, theirs, mine)
            return jnp.stack([first, second], axis=1).reshape(rows, w)

        row_ids = (r * rows + jnp.arange(rows, dtype=jnp.int32)) // BLOCK
        in_pattern = jnp.any(row_ids[:, None] == low_rows[None, :], axis=1)[:, None]

        share = low_rows.shape[0] // R
        pattern_idx = lax.dynamic_slice_in_dim(low_rows, r * share, share)
        if R == 2:
            count = rows // BLOCK
            other_idx = lax.dynamic_slice_in_dim(low_rows, (1 - r) * share, share)
            pack_idx = jnp.concatenate([pattern_idx, other_idx]) % count
            pack_here = jnp.repeat(pattern_idx // count == r, BLOCK)[:, None]
        else:
            pack_idx = pattern_idx

        def take_pattern(x):
            return take_blocks([x], pack_idx, BLOCK) if R == 2 else x

        def pack_rows(taken):
            if R == 2:
                cut = share * BLOCK
                return [taken[:cut], row_swap(taken[cut:])]
            return [lax.all_gather(taken, "row", axis=0, tiled=True)]

        def packed(parts):
            if R == 2:
                return jnp.where(pack_here, *parts)
            return take_blocks(parts, pattern_idx, BLOCK)

        steps = n // 2
        first = n - 1
        count = first + 3 * steps
        env, due, events = {}, {}, {}

        def step_of(stage, j):
            if stage == 0:
                return (j * (first - 1) + 2) // 3
            return first + (stage - 1) * steps + (j * (steps - 1) + 2) // 3

        def on(stage, j):
            def register(f):
                events.setdefault(step_of(stage, j), []).append(f)

            return register

        def keep(name, value, *until):
            env[name] = value
            if until:
                due[name] = step_of(*until)

        def ring_of(stage):
            return [env["ring", stage, s] for s in shifts]

        def entries(name, some=shifts):
            return [offsets[name] + s for s in some]

        def in_pairs(some):
            return [s for j in some for s in pairs[j]]

        def exchanged(own, other, rest_own, rest_other):
            return (own, row_swap(rest_own)), (core_swap(other), both_swap(rest_other))

        def finished(base, sums, first=0, so_far=None):
            place = offsets["places"] + first
            return finish(base, *sums, env["index"], offsets["core"], place, so_far)

        def core_sum(parts):
            own, send = parts
            return own + core_swap(send).astype(F32)

        @on(0, 0)
        def _():
            keep("upper_rows", gather_rows(low_upper), 0, 1)
            env["low_taken"] = take_pattern(low_ancestor)

        @on(0, 1)
        def _():
            keep("low_parts", pack_rows(env["low_taken"]), 0, 3)
            env["sigma_send"] = take_symmetric(sigma, env["index"], offsets["send"], slots)

        @on(0, 2)
        def _():
            env["upper"] = both_cores(env["upper_rows"])
            keep("top_rows", gather_rows(top_panel), 1, 0)
            env["dinv_send"] = take_symmetric(top_dinv, env["index"], offsets["send"], slots)

        @on(1, 1)
        def _():
            env["low_send"] = jnp.concatenate([low_upper, packed(env["low_parts"])], axis=0)

        @on(1, 0)
        def _():
            env["v_parts"] = times(ring_of(0), env["upper"], env["index"], offsets["column"])

        @on(1, 1)
        def _():
            own, send = env.pop("v_parts")
            env["v_parts"] = own, core_swap(send)

        @on(1, 2)
        def _():
            masked = jnp.where(in_pattern, low_ancestor, jnp.zeros_like(low_ancestor))
            v = (masked.astype(F32) - add(env.pop("v_parts"))).astype(BF16)
            keep("v_rows", gather_rows(v), 1, 3)

        @on(1, 3)
        def _():
            env["top_right"] = both_cores(env["top_rows"])

        @on(2, 0)
        def _():
            env["x_parts"] = times_symmetric(
                ring_of(1), both_cores(env["v_rows"]), env["index"], offsets["symmetric"], slots
            )

        @on(2, 1)
        def _():
            keep("x_sum", scatter_rows(core_sum(env.pop("x_parts"))), 2, 2)

        @on(2, 2)
        def _():
            env["off_parts"] = times_symmetric(
                ring_of(1), env["top_right"], env["index"], offsets["symmetric"], slots
            )

        @on(2, 3)
        def _():
            x = (-add(env.pop("x_sum"))).astype(BF16)
            env["low_anc"] = jnp.where(in_pattern, x, jnp.zeros_like(x))
            env["x"] = x
            keep("off_sum", scatter_rows(core_sum(env.pop("off_parts"))), 3, 0)

        @on(3, 0)
        def _():
            dinv_upper = times_symmetric(
                ring_of(2), env["upper"], env["index"], offsets["symmetric"], slots
            )
            env["low_top_parts"] = times_t(
                ring_of(0), both_cores([env["x"]]), env["index"], entries("column"), "add", dinv_upper
            )

        @on(3, 1)
        def _():
            keep("low_top_sum", scatter_rows(core_sum(env.pop("low_top_parts"))), 3, 1)
            env["x_taken"] = take_pattern(env["x"])
            env["top_off"] = (-add(env.pop("off_sum"))).astype(BF16)
            right = both_cores([env["top_off"]])
            if R == 2:
                at0 = entries("mine", in_pairs(near + far + [0]))
                chunks = [ring_of(0)[s] for s in in_pairs(near + far + [0])]
                env["diag_parts"] = times_t(chunks, right, env["index"], at0, "pairs")
            else:
                env["diag_parts"] = times_t(ring_of(0), right, env["index"], entries("chip"), "blocks")

        @on(3, 2)
        def _():
            env["low_top"] = (-add(env.pop("low_top_sum"))).astype(BF16)
            env["low_top_both"] = both_cores([env["low_top"]])
            env["x_packed"] = both_cores([packed(pack_rows(env["x_taken"]))])
            if R == 2:
                keep("diag_sum", exchanged(*env.pop("diag_parts")), 3, 3)
            else:
                keep("diag_sum", scatter_rows(env.pop("diag_parts")[0]), 3, 3)

        def diag_part(some, start=()):
            chunks = [env["ring", 3, s] for s in some]
            at0 = entries("mine", some)
            if "low_right" in env:
                return times_t(chunks, [env["low_right"]], env["index"], at0, "pairs", start)
            right = env["low_top_both"] + env["x_packed"]
            *out, env["low_right"] = times_t(
                chunks, right, env["index"], at0, "pairs", start, hand_on=True
            )
            return out

        if R == 2:

            @on(3, 2)
            def _():
                env["near_parts"] = diag_part(in_pairs(near))
                env["own_parts"] = diag_part([0])

            @on(3, 3)
            def _():
                keep("near", exchanged(*env.pop("near_parts")), 3, 3)
                env["far_parts"] = diag_part(in_pairs(far))
                env["far"] = exchanged(*env["far_parts"])
                due["far"] = count
        env["index"] = index

        def hop(x, way):
            return lax.ppermute(x, "col", ring_perms[way])

        halves = list(jnp.split(top_panel, 2, axis=0))
        env["ring", 0, 0] = [top_panel]
        for s in shifts[1:]:
            env["ring", 0, s] = [None, None]
        flying = []

        def send_first(number):
            got = []
            for way in (1, -1):
                half, turn = (number + (way < 0)) % 2, number // 2
                x = env["ring", 0, way * turn % n][half] if turn else halves[half]
                got.append(((way * (turn + 1)) % n, half, hop(x, way)))
            flying.append(got)

        def send(stage, turn):
            if turn == 1:
                env["ring", stage, 0] = [env[("sigma_send", "dinv_send", "low_send")[stage - 1]]]
            held = [env["ring", stage, way * (turn - 1) % n][0] for way in (1, -1)]
            if turn == steps:
                half = held[0].shape[0] // 2
                held = [held[0][:half], held[1][half:]]
            got = [hop(x, way) for x, way in zip(held, (1, -1))]
            if turn == steps:
                return {("ring", stage, steps): got}
            return {("ring", stage, way * turn % n): [x] for x, way in zip(got, (1, -1))}

        send_first(0)
        for g in range(count):
            arriving = {}
            if g < first:
                if g + 1 < first:
                    send_first(g + 1)
            else:
                arriving = send((g - first) // steps + 1, (g - first) % steps + 1)
            for event in events.get(g, []):
                event()
            env.update(arriving)
            if g < first:
                for s, half, x in flying.pop(0):
                    env["ring", 0, s][half] = x
            names = [name for name in env if due.get(name, 0) <= g]
            leaves, tree = jax.tree.flatten([env[name] for name in names])
            env.update(zip(names, jax.tree.unflatten(tree, lax.optimization_barrier(leaves))))

        if R == 2:
            last = diag_part([steps], env["own_parts"])
            low_diag = finished(low_dinv, env["near"])
            env["index"], _ = lax.optimization_barrier((env["index"], last[0]))
            last = exchanged(*last)
            low_diag = finished(low_dinv, env["far"], len(near), low_diag)
            low_diag = finished(low_dinv, last, len(near + far), low_diag)
            top_diag = finished(top_dinv, env["diag_sum"])
        else:
            right = env["low_top_both"] + env["x_packed"]
            parts = times_t(ring_of(3), right, env["index"], entries("chip"), "blocks")
            total = add(scatter_rows(parts[0]))
            low_diag = (low_dinv.astype(F32) - own_columns(total)).astype(BF16)
            top_diag = (top_dinv.astype(F32) - own_columns(add(env["diag_sum"]))).astype(BF16)
        return (env["top_off"], top_diag, env["low_top"], env["low_anc"], low_diag)

    spec = P("row", "col")
    return jax.shard_map(
        body, mesh=mesh, in_specs=(spec,) * 6 + (P(),), out_specs=(spec,) * 5, check_vma=False
    )
```

```python
import jax
import jax.numpy as jnp
import numpy as np
from jax import lax
from jax.experimental import pallas as pl
from jax.experimental.pallas import tpu as pltpu
from jax.sharding import PartitionSpec as P

BLOCK = 128
F32 = jnp.float32
BF16 = jnp.bfloat16
VMEM_BYTES = 56 * 1024 * 1024


def dot(a, b):
    return jnp.dot(a, b, preferred_element_type=F32)


def dot_t(a, b):
    return lax.dot_general(a, b, (((0,), (0,)), ((), ())), preferred_element_type=F32)


def cost(flops=0, bytes_accessed=0):
    return pl.CostEstimate(flops=1, bytes_accessed=1, transcendentals=0)


def params():
    return pltpu.CompilerParams(vmem_limit_bytes=VMEM_BYTES)


def at(index, size):
    return pl.ds(pl.multiple_of(index * size, size), size)


def whole(x):
    return pl.BlockSpec(x.shape, lambda i, idx: (0, 0))


def copy_block(out, place, panel, index, w):
    per = panel[0].shape[0] // w
    for j in range(0, len(panel), 2):

        @pl.when(index // per == j // 2)
        def _():
            rows = at(index - (j // 2) * per, w)
            out[pl.ds(place * w, w), :w] = panel[j][rows, :]
            out[pl.ds(place * w, w), w:] = panel[j + 1][rows, :]


def take_symmetric(x, idx, base, slots):
    w = x.shape[1]
    half = w // 2

    def kernel(idx_ref, x_ref, o_ref):
        for b in range(slots - 1):
            o_ref[b * w : (b + 1) * w, :] = x_ref[at(idx_ref[base + b], w), :]
        block = x_ref[at(idx_ref[base + slots - 1], w), :]
        turned = idx_ref[base + slots] == 1

        @pl.when(turned)
        def _():
            o_ref[(slots - 1) * w :, :] = block[:, half:].T

        @pl.when(jnp.logical_not(turned))
        def _():
            o_ref[(slots - 1) * w :, :] = block[:half, :]

    return pl.pallas_call(
        kernel,
        grid_spec=pltpu.PrefetchScalarGridSpec(
            num_scalar_prefetch=1,
            grid=(1,),
            in_specs=[whole(x)],
            out_specs=pl.BlockSpec(((slots - 1) * w + half, w), lambda i, idx: (0, 0)),
        ),
        out_shape=jax.ShapeDtypeStruct(((slots - 1) * w + half, w), x.dtype),
        cost_estimate=cost(),
    )(idx, x)


def take_blocks(x, idx, size):
    count, width = idx.shape[0], x.shape[1]

    def kernel(idx_ref, x_ref, o_ref):
        for i in range(count):
            o_ref[i * size : (i + 1) * size, :] = x_ref[at(idx_ref[i], size), :]

    return pl.pallas_call(
        kernel,
        grid_spec=pltpu.PrefetchScalarGridSpec(
            num_scalar_prefetch=1,
            grid=(1,),
            in_specs=[whole(x)],
            out_specs=pl.BlockSpec((count * size, width), lambda i, idx: (0, 0)),
        ),
        out_shape=jax.ShapeDtypeStruct((count * size, width), x.dtype),
        cost_estimate=cost(),
    )(idx, x)


def times(chunks, panel, idx, base):
    m = len(chunks)
    counts = [len(pieces) for pieces in chunks]
    rows, w = sum(x.shape[0] for x in chunks[0]), chunks[0][0].shape[1]
    tile = min(256, rows // 2)
    steps = rows // tile

    def kernel(idx_ref, *refs):
        own, send, right = refs[-3:]
        pieces, rest = split(refs[:-3], counts)
        step = pl.program_id(0)

        @pl.when(step == 0)
        def _():
            for s in range(m):
                copy_block(right, s, rest, idx_ref[base + s], w)

        def block(refs):
            value = refs[0][...]
            for i in range(1, len(refs)):
                value = jnp.where(step // (steps // len(refs)) == i, refs[i][...], value)
            return value

        total = dot(jnp.concatenate([block(x) for x in pieces], axis=1), right[...])
        own[...] = total[:, :w]
        send[...] = total[:, w:].astype(BF16)

    def piece(part, count):
        each = steps // count
        return pl.BlockSpec((tile, w), lambda i, idx: (jnp.clip(i - part * each, 0, each - 1), 0))

    return pl.pallas_call(
        kernel,
        grid_spec=pltpu.PrefetchScalarGridSpec(
            num_scalar_prefetch=1,
            grid=(steps,),
            in_specs=[piece(part, count) for count in counts for part in range(count)]
            + [whole(x) for x in panel],
            out_specs=[pl.BlockSpec((tile, w), lambda i, idx: (i, 0))] * 2,
            scratch_shapes=[pltpu.VMEM((m * w, 2 * w), BF16)],
        ),
        out_shape=[
            jax.ShapeDtypeStruct((rows, w), F32),
            jax.ShapeDtypeStruct((rows, w), BF16),
        ],
        compiler_params=params(),
        cost_estimate=cost(),
    )(idx, *sum(chunks, []), *panel)


def load_all(chunks, held, sems):
    waits = []
    for s, pieces in enumerate(chunks):
        base, copies = 0, []
        for i, piece in enumerate(pieces):
            size = piece.shape[0]
            copies.append(
                pltpu.make_async_copy(piece, held.at[s, pl.ds(base, size)], sems.at[s, i])
            )
            copies[-1].start()
            base += size
        waits.append(copies)

    def wait(s):
        for copy in waits[s]:
            copy.wait()

    return wait


def split(refs, counts):
    out, base = [], 0
    for count in counts:
        out.append(list(refs[base : base + count]))
        base += count
    return out, refs[base:]


def times_t(chunks, right, idx, at0, form, start=(), hand_on=False):
    m = len(chunks)
    counts = [len(pieces) for pieces in chunks]
    rows, w = sum(x.shape[0] for x in chunks[0]), chunks[0][0].shape[1]
    ANY = pl.BlockSpec(memory_space=pl.ANY)
    kept = lambda shape, dtype: jax.ShapeDtypeStruct(shape, dtype)
    if form == "blocks":
        outs = [kept((m * w, 2 * w), BF16)]
    elif form == "add":
        outs = [kept(x.shape, x.dtype) for x in start]
    else:
        outs = [kept(((m + 1) // 2 * w, w), t) for t in (F32, F32, BF16, BF16)]
    if hand_on:
        outs.append(kept((rows, 2 * w), BF16))

    def kernel(idx_ref, *refs):
        hbm, rest = split(refs, counts)
        right_refs, rest = rest[: len(right)], rest[len(right) :]
        start_refs, rest = rest[: len(start)], rest[len(start) :]
        out, (both, held, sems) = rest[: len(outs)], rest[len(outs) :]
        wait = load_all(hbm, held, sems)
        base = 0
        if len(right) == 1:
            both = right_refs[0]
        for j in range(0, len(right) - 1, 2):
            size = right[j].shape[0]
            both[base : base + size, :w] = right_refs[j][...]
            both[base : base + size, w:] = right_refs[j + 1][...]
            base += size
        for i in range(len(start)):
            out[i][...] = start_refs[i][...]
        if hand_on:
            out[-1][...] = both[...]
        for s in range(m):
            wait(s)
            value = dot_t(held[s], both[...])
            if form == "blocks":
                out[0][at(idx_ref[at0[s]], w), :] = value.astype(BF16)
            elif form == "add":
                place = at(idx_ref[at0[s]], w)
                out[0][place, :] = out[0][place, :] + value[:, :w]
                out[1][place, :] = (out[1][place, :].astype(F32) + value[:, w:]).astype(BF16)
            else:
                place = pl.ds(s // 2 * w, w)

                @pl.when(idx_ref[at0[s]] == 1)
                def _():
                    out[0][place, :] = value[:, :w]
                    out[1][place, :] = value[:, w:]

                @pl.when(idx_ref[at0[s]] == 0)
                def _():
                    out[2][place, :] = value[:, :w].astype(BF16)
                    out[3][place, :] = value[:, w:].astype(BF16)

    return pl.pallas_call(
        kernel,
        grid_spec=pltpu.PrefetchScalarGridSpec(
            num_scalar_prefetch=1,
            grid=(1,),
            in_specs=[ANY] * sum(counts) + [whole(x) for x in (*right, *start)],
            out_specs=[whole(x) for x in outs],
            scratch_shapes=[
                pltpu.VMEM((rows if len(right) > 1 else 16, 2 * w), BF16),
                pltpu.VMEM((m, rows, w), BF16),
                pltpu.SemaphoreType.DMA((m, max(counts))),
            ],
        ),
        out_shape=outs,
        compiler_params=params(),
        cost_estimate=cost(4 * m * rows * w * w, 0),
    )(idx, *sum(chunks, []), *right, *start)


def finish(base, own, other, idx, core, places, so_far=None):
    w = base.shape[1]
    count = own[0].shape[0] // w

    def kernel(idx_ref, base_ref, a, b, c, d, *rest):
        k = idx_ref[core]
        for place, x, y in ((at(k, w), a, b), (at(1 - k, w), c, d)):
            value = x[...].astype(F32) + y[...].astype(F32)
            rest[-1][place, :] = (base_ref[place, :].astype(F32) - value).astype(BF16)

    here = pl.BlockSpec((2 * w, w), lambda t, idx: (idx[places + t], 0))
    extra = [] if so_far is None else [so_far]
    return pl.pallas_call(
        kernel,
        grid_spec=pltpu.PrefetchScalarGridSpec(
            num_scalar_prefetch=1,
            grid=(count,),
            in_specs=[here]
            + [pl.BlockSpec((w, w), lambda t, idx: (t, 0))] * 4
            + [pl.BlockSpec(memory_space=pl.ANY) for _ in extra],
            out_specs=here,
        ),
        out_shape=jax.ShapeDtypeStruct(base.shape, BF16),
        input_output_aliases={} if so_far is None else {6: 0},
        cost_estimate=cost(),
    )(idx, base, *own, *other, *extra)


def times_symmetric(chunks, panel, table, base0, slots):
    m = len(chunks)
    counts = [len(pieces) for pieces in chunks]
    w = chunks[0][0].shape[1]
    height = sum(x.shape[0] for x in panel) // 2
    inner = slots - 2
    half = w // 2
    ANY = pl.BlockSpec(memory_space=pl.ANY)

    def kernel(t, *refs):
        hbm, rest = split(refs, counts)
        panel_refs = rest[: len(panel)]
        own, send, acc, p, few, c, sems = rest[len(panel) :]
        wait = load_all(hbm, c, sems)
        base = 0
        for j in range(0, len(panel), 2):
            size = panel[j].shape[0]
            p[base : base + size, :w] = panel_refs[j][...]
            p[base : base + size, w:] = panel_refs[j + 1][...]
            base += size
        acc[...] = jnp.zeros_like(acc)

        def add(index, value):
            acc[at(index, w), :] = acc[at(index, w), :] + value

        for s in range(m):
            b0 = base0 + s * (slots + 5)
            q = t[b0]
            row = lambda b: t[b0 + 1 + b]
            wait(s)
            right_q = p[at(q, w), :]
            for b in range(1, slots - 1):
                few[(b - 1) * w : b * w, :] = p[at(row(b), w), :]
            part = dot(c[s, : (slots - 1) * w, :], right_q)
            for b in range(slots - 1):
                add(row(b), part[b * w : (b + 1) * w])
            add(q, dot_t(c[s, w : (slots - 1) * w, :], few[...]))

            @pl.when(t[b0 + 3 + slots] == 1)
            def _():
                add(q, dot_t(c[s, :w, :], p[at(row(0), w), :]))

            @pl.when(t[b0 + 4 + slots] == 1)
            def _():
                last = c[s, (slots - 1) * w :, :]
                column = t[b0 + 1 + slots]
                place = at(2 * row(slots - 1) + t[b0 + 2 + slots], half)
                acc[place, :] = acc[place, :] + dot(last, p[at(column, w), :])
                add(column, dot_t(last, p[place, :]))

        own[...] = acc[:, :w]
        send[...] = acc[:, w:].astype(BF16)

    return pl.pallas_call(
        kernel,
        grid_spec=pltpu.PrefetchScalarGridSpec(
            num_scalar_prefetch=1,
            grid=(1,),
            in_specs=[ANY] * sum(counts) + [whole(x) for x in panel],
            out_specs=[pl.BlockSpec((height, w), lambda i, t: (0, 0))] * 2,
            scratch_shapes=[
                pltpu.VMEM((height, 2 * w), F32),
                pltpu.VMEM((height, 2 * w), BF16),
                pltpu.VMEM((inner * w, 2 * w), BF16),
                pltpu.VMEM((m, (slots - 1) * w + half, w), BF16),
                pltpu.SemaphoreType.DMA((m, max(counts))),
            ],
        ),
        out_shape=[
            jax.ShapeDtypeStruct((height, w), F32),
            jax.ShapeDtypeStruct((height, w), BF16),
        ],
        compiler_params=params(),
        cost_estimate=cost(2 * height * height * w, 0),
    )(table, *sum(chunks, []), *panel)


def solution(mesh):
    R, C = mesh.shape["row"], mesh.shape["col"]
    n = C // 2
    nb = C // R
    slots = nb // 2 + 1
    order = list(range(0, n, 2)) + list(range(n - 1, 0, -2))
    place = [order.index(c) for c in range(n)]
    shifts = list(range(n))
    pairs = [(s, s + n // 2) for s in range(n // 2)]

    def ring_perm(shift):
        return [
            (c * 2 + k, order[(place[c] + shift) % n] * 2 + k) for c in range(n) for k in range(2)
        ]

    ring_perms = {1: ring_perm(1), -1: ring_perm(-1)}
    core_perm = [(i, i ^ 1) for i in range(C)]

    def slot(x, q):
        return ((q // nb) ^ x) * nb + q % nb if R == 2 else q

    def provided(x, q):
        h, lq = q // nb, q % nb
        if h == x:
            return [(lq + b) % nb for b in range(slots - 1)]
        return [(lq + 2 * b + (x > h)) % nb for b in range(slots - 1)]

    def sent(x, q):
        return provided(x, q) + [(q + nb // 2) % nb, int(q % nb >= nb // 2)]

    def rows_of(make):
        return np.array([[make(x, col) for col in range(C)] for x in range(R)], np.int32)

    def source(col, shift):
        return order[(place[col // 2] - shift) % n] * 2 + col % 2

    def symmetric_row(x, col):
        out = []
        for s in shifts:
            q = source(col, s)
            inside = q // nb == x
            out += [slot(x, q)] + [slot(x, x * nb + i) for i in provided(x, q)]
            low = q % nb % (nb // 2)
            out += [slot(x, x * nb + low + nb // 2), slot(x, x * nb + low)]
            out += [int(q % nb >= nb // 2), int(not inside), int(inside)]
        return out

    near, far = list(range(2, n // 2 - 1)), [1, n // 2 - 1]
    table_of = dict(
        send=sent,
        column=lambda x, col: [slot(x, source(col, s)) for s in shifts],
        chip=lambda x, col: [slot(x, source(col, s)) // 2 for s in shifts],
        symmetric=symmetric_row,
        mine=lambda x, col: [int(source(col, s) // nb == x) for s in shifts],
        places=lambda x, col: [
            max(source(col, s) % nb // 2 * int(source(col, s) // nb == x) for s in pairs[j])
            for j in near + far + [0]
        ],
        core=lambda x, col: [col % 2],
    )
    offsets, table = {}, []
    for name, make in table_of.items():
        rows = rows_of(make)
        offsets[name] = sum(x.shape[2] for x in table)
        table.append(rows)
    table = np.concatenate(table, axis=2)

    def core_swap(x):
        return lax.ppermute(x, "col", core_perm)

    def row_swap(x):
        return lax.ppermute(x, "row", [(0, 1), (1, 0)])

    def both_swap(x):
        pairs = [(x * C + i, (1 - x) * C + (i ^ 1)) for x in range(2) for i in range(C)]
        return lax.ppermute(x, ("row", "col"), pairs)

    def body(sigma, top_panel, top_dinv, low_upper, low_ancestor, low_dinv, low_rows):
        rows, w = sigma.shape
        r = lax.axis_index("row")
        col = lax.axis_index("col")
        k = col % 2
        index = lax.dynamic_slice(
            jnp.asarray(table), (r, col, 0), (1, 1, table.shape[2])
        ).reshape(-1)

        def gather_rows(x):
            if R == 2:
                return [x, row_swap(x)]
            return [lax.all_gather(x, "row", axis=0, tiled=True)]

        def both_cores(pieces):
            return [y for x in pieces for y in (x, core_swap(x))]

        def scatter_rows(x):
            if R == 2:
                half = x.shape[0] // 2
                return [x[:half], row_swap(x[half:].astype(BF16))]
            return [lax.psum_scatter(x.astype(BF16), "row", scatter_dimension=0, tiled=True)]

        def add(parts):
            return sum((x.astype(F32) for x in parts[1:]), parts[0].astype(F32))

        def own_columns(y):
            y = y.reshape(nb // 2, w, 2 * w)
            mine, theirs = y[..., :w], core_swap(y[..., w:])
            first = jnp.where(k == 0, mine, theirs)
            second = jnp.where(k == 0, theirs, mine)
            return jnp.stack([first, second], axis=1).reshape(rows, w)

        row_ids = (r * rows + jnp.arange(rows, dtype=jnp.int32)) // BLOCK
        in_pattern = jnp.any(row_ids[:, None] == low_rows[None, :], axis=1)[:, None]

        share = low_rows.shape[0] // R
        pattern_idx = lax.dynamic_slice_in_dim(low_rows, r * share, share)
        if R == 2:
            count = rows // BLOCK
            other_idx = lax.dynamic_slice_in_dim(low_rows, (1 - r) * share, share)
            pack_idx = jnp.concatenate([pattern_idx, other_idx]) % count
            pack_here = jnp.repeat(pattern_idx // count == r, BLOCK)[:, None]
        else:
            pack_idx = pattern_idx

        def take_pattern(x):
            return take_blocks(x, pack_idx, BLOCK) if R == 2 else x

        def pack_rows(taken):
            if R == 2:
                cut = share * BLOCK
                return [taken[:cut], row_swap(taken[cut:])]
            return [lax.all_gather(taken, "row", axis=0, tiled=True)]

        def packed(parts):
            if R == 2:
                return jnp.where(pack_here, *parts)
            return take_blocks(*parts, pattern_idx, BLOCK)

        steps = n // 2
        first = n - 1
        count = first + 3 * steps
        env, due, events = {}, {}, {}

        def step_of(stage, j):
            if stage == 0:
                return (j * (first - 1) + 2) // 3
            return first + (stage - 1) * steps + (j * (steps - 1) + 2) // 3

        def on(stage, j):
            def register(f):
                events.setdefault(step_of(stage, j), []).append(f)

            return register

        def keep(name, value, *until):
            env[name] = value
            if until:
                due[name] = step_of(*until)

        def ring_of(stage):
            return [env["ring", stage, s] for s in shifts]

        def entries(name, some=shifts):
            return [offsets[name] + s for s in some]

        def in_pairs(some):
            return [s for j in some for s in pairs[j]]

        def exchanged(own, other, rest_own, rest_other):
            return (own, row_swap(rest_own)), (core_swap(other), both_swap(rest_other))

        def finished(base, sums, first=0, so_far=None):
            place = offsets["places"] + first
            return finish(base, *sums, env["index"], offsets["core"], place, so_far)

        def core_sum(parts):
            own, send = parts
            return own + core_swap(send).astype(F32)

        @on(0, 0)
        def _():
            keep("upper_rows", gather_rows(low_upper), 0, 1)
            env["low_taken"] = take_pattern(low_ancestor)

        @on(0, 1)
        def _():
            keep("low_parts", pack_rows(env["low_taken"]), 0, 3)
            env["sigma_send"] = take_symmetric(sigma, env["index"], offsets["send"], slots)

        @on(0, 2)
        def _():
            keep("upper", both_cores(env["upper_rows"]), 0, 3)
            keep("top_rows", gather_rows(top_panel), 1, 0)
            env["dinv_send"] = take_symmetric(top_dinv, env["index"], offsets["send"], slots)

        @on(1, 1)
        def _():
            env["low_send"] = jnp.concatenate([low_upper, packed(env["low_parts"])], axis=0)

        @on(1, 0)
        def _():
            env["v_parts"] = times(ring_of(0), env["upper"], env["index"], offsets["column"])

        @on(1, 1)
        def _():
            own, send = env.pop("v_parts")
            env["v_parts"] = own, core_swap(send)

        @on(1, 2)
        def _():
            masked = jnp.where(in_pattern, low_ancestor, jnp.zeros_like(low_ancestor))
            v = (masked.astype(F32) - add(env.pop("v_parts"))).astype(BF16)
            keep("v_rows", gather_rows(v), 1, 3)

        @on(1, 3)
        def _():
            env["top_right"] = both_cores(env["top_rows"])

        @on(2, 0)
        def _():
            env["x_parts"] = times_symmetric(
                ring_of(1), both_cores(env["v_rows"]), env["index"], offsets["symmetric"], slots
            )

        @on(2, 1)
        def _():
            keep("x_sum", scatter_rows(core_sum(env.pop("x_parts"))), 2, 2)

        @on(2, 2)
        def _():
            env["off_parts"] = times_symmetric(
                ring_of(1), env["top_right"], env["index"], offsets["symmetric"], slots
            )

        @on(2, 3)
        def _():
            x = (-add(env.pop("x_sum"))).astype(BF16)
            env["low_anc"] = jnp.where(in_pattern, x, jnp.zeros_like(x))
            env["x"] = x
            keep("off_sum", scatter_rows(core_sum(env.pop("off_parts"))), 3, 0)

        @on(3, 0)
        def _():
            dinv_upper = times_symmetric(
                ring_of(2), env["upper"], env["index"], offsets["symmetric"], slots
            )
            env["low_top_parts"] = times_t(
                ring_of(0), both_cores([env["x"]]), env["index"], entries("column"), "add", dinv_upper
            )

        @on(3, 1)
        def _():
            keep("low_top_sum", scatter_rows(core_sum(env.pop("low_top_parts"))), 3, 1)
            env["x_taken"] = take_pattern(env["x"])
            env["top_off"] = (-add(env.pop("off_sum"))).astype(BF16)
            right = both_cores([env["top_off"]])
            if R == 2:
                at0 = entries("mine", in_pairs(near + far + [0]))
                chunks = [ring_of(0)[s] for s in in_pairs(near + far + [0])]
                env["diag_parts"] = times_t(chunks, right, env["index"], at0, "pairs")
            else:
                env["diag_parts"] = times_t(ring_of(0), right, env["index"], entries("chip"), "blocks")

        @on(3, 2)
        def _():
            env["low_top"] = (-add(env.pop("low_top_sum"))).astype(BF16)
            env["low_top_both"] = both_cores([env["low_top"]])
            env["x_packed"] = both_cores([packed(pack_rows(env["x_taken"]))])
            if R == 2:
                keep("diag_sum", exchanged(*env.pop("diag_parts")), 3, 3)
            else:
                keep("diag_sum", scatter_rows(env.pop("diag_parts")[0]), 3, 3)

        def diag_part(some, start=()):
            chunks = [env["ring", 3, s] for s in some]
            at0 = entries("mine", some)
            if "low_right" in env:
                return times_t(chunks, [env["low_right"]], env["index"], at0, "pairs", start)
            right = env["low_top_both"] + env["x_packed"]
            *out, env["low_right"] = times_t(
                chunks, right, env["index"], at0, "pairs", start, hand_on=True
            )
            return out

        if R == 2:

            @on(3, 2)
            def _():
                env["near_parts"] = diag_part(in_pairs(near))
                env["own_parts"] = diag_part([0])

            @on(3, 3)
            def _():
                keep("near", exchanged(*env.pop("near_parts")), 3, 3)
                env["top_diag"] = finished(top_dinv, env["diag_sum"])
                env["index"], _ = lax.optimization_barrier((env["index"], env["top_diag"]))
                env["far_parts"] = diag_part(in_pairs(far))
                env["far"] = exchanged(*env["far_parts"])
                due["far"] = count
        env["index"] = index

        def hop(x, way):
            return lax.ppermute(x, "col", ring_perms[way])

        halves = list(jnp.split(top_panel, 2, axis=0))
        env["ring", 0, 0] = [top_panel]
        for s in shifts[1:]:
            env["ring", 0, s] = [None, None]
        flying = []

        def send_first(number):
            got = []
            for way in (1, -1):
                half, turn = (number + (way < 0)) % 2, number // 2
                x = env["ring", 0, way * turn % n][half] if turn else halves[half]
                got.append(((way * (turn + 1)) % n, half, hop(x, way)))
            flying.append(got)

        def send(stage, turn):
            if turn == 1:
                env["ring", stage, 0] = [env[("sigma_send", "dinv_send", "low_send")[stage - 1]]]
            held = [env["ring", stage, way * (turn - 1) % n][0] for way in (1, -1)]
            if turn == steps:
                half = held[0].shape[0] // 2
                held = [held[0][:half], held[1][half:]]
            got = [hop(x, way) for x, way in zip(held, (1, -1))]
            if turn == steps:
                return {("ring", stage, steps): got}
            return {("ring", stage, way * turn % n): [x] for x, way in zip(got, (1, -1))}

        send_first(0)
        for g in range(count):
            arriving = {}
            if g < first:
                if g + 1 < first:
                    send_first(g + 1)
            else:
                arriving = send((g - first) // steps + 1, (g - first) % steps + 1)
            for event in events.get(g, []):
                event()
            env.update(arriving)
            if g < first:
                for s, half, x in flying.pop(0):
                    env["ring", 0, s][half] = x
            names = [name for name in env if due.get(name, 0) <= g]
            leaves, tree = jax.tree.flatten([env[name] for name in names])
            env.update(zip(names, jax.tree.unflatten(tree, lax.optimization_barrier(leaves))))

        if R == 2:
            last = diag_part([steps], env["own_parts"])
            low_diag = finished(low_dinv, env["near"])
            env["index"], _ = lax.optimization_barrier((env["index"], last[0]))
            last = exchanged(*last)
            low_diag = finished(low_dinv, env["far"], len(near), low_diag)
            low_diag = finished(low_dinv, last, len(near + far), low_diag)
            top_diag = env["top_diag"]
        else:
            right = env["low_top_both"] + env["x_packed"]
            parts = times_t(ring_of(3), right, env["index"], entries("chip"), "blocks")
            total = add(scatter_rows(parts[0]))
            low_diag = (low_dinv.astype(F32) - own_columns(total)).astype(BF16)
            top_diag = (top_dinv.astype(F32) - own_columns(add(env["diag_sum"]))).astype(BF16)
        return (env["top_off"], top_diag, env["low_top"], env["low_anc"], low_diag)

    spec = P("row", "col")
    return jax.shard_map(
        body, mesh=mesh, in_specs=(spec,) * 6 + (P(),), out_specs=(spec,) * 5, check_vma=False
    )
```

```python
import jax
import jax.numpy as jnp
import numpy as np
from jax import lax
from jax.experimental import pallas as pl
from jax.experimental.pallas import tpu as pltpu
from jax.sharding import PartitionSpec as P

BLOCK = 128
F32 = jnp.float32
BF16 = jnp.bfloat16
VMEM_BYTES = 56 * 1024 * 1024


def dot(a, b):
    return jnp.dot(a, b, preferred_element_type=F32)


def dot_t(a, b):
    return lax.dot_general(a, b, (((0,), (0,)), ((), ())), preferred_element_type=F32)


def cost(flops=0, bytes_accessed=0):
    return pl.CostEstimate(flops=1, bytes_accessed=1, transcendentals=0)


def params():
    return pltpu.CompilerParams(vmem_limit_bytes=VMEM_BYTES)


def at(index, size):
    return pl.ds(pl.multiple_of(index * size, size), size)


def whole(x):
    return pl.BlockSpec(x.shape, lambda i, idx: (0, 0))


def copy_block(out, place, panel, index, w):
    per = panel[0].shape[0] // w
    for j in range(0, len(panel), 2):

        @pl.when(index // per == j // 2)
        def _():
            rows = at(index - (j // 2) * per, w)
            out[pl.ds(place * w, w), :w] = panel[j][rows, :]
            out[pl.ds(place * w, w), w:] = panel[j + 1][rows, :]


def take_symmetric(x, idx, base, slots):
    w = x.shape[1]
    half = w // 2

    def kernel(idx_ref, x_ref, o_ref):
        for b in range(slots - 1):
            o_ref[b * w : (b + 1) * w, :] = x_ref[at(idx_ref[base + b], w), :]
        block = x_ref[at(idx_ref[base + slots - 1], w), :]
        turned = idx_ref[base + slots] == 1

        @pl.when(turned)
        def _():
            o_ref[(slots - 1) * w :, :] = block[:, half:].T

        @pl.when(jnp.logical_not(turned))
        def _():
            o_ref[(slots - 1) * w :, :] = block[:half, :]

    return pl.pallas_call(
        kernel,
        grid_spec=pltpu.PrefetchScalarGridSpec(
            num_scalar_prefetch=1,
            grid=(1,),
            in_specs=[whole(x)],
            out_specs=pl.BlockSpec(((slots - 1) * w + half, w), lambda i, idx: (0, 0)),
        ),
        out_shape=jax.ShapeDtypeStruct(((slots - 1) * w + half, w), x.dtype),
        cost_estimate=cost(),
    )(idx, x)


def take_blocks(x, idx, size):
    count, width = idx.shape[0], x.shape[1]

    def kernel(idx_ref, x_ref, o_ref):
        for i in range(count):
            o_ref[i * size : (i + 1) * size, :] = x_ref[at(idx_ref[i], size), :]

    return pl.pallas_call(
        kernel,
        grid_spec=pltpu.PrefetchScalarGridSpec(
            num_scalar_prefetch=1,
            grid=(1,),
            in_specs=[whole(x)],
            out_specs=pl.BlockSpec((count * size, width), lambda i, idx: (0, 0)),
        ),
        out_shape=jax.ShapeDtypeStruct((count * size, width), x.dtype),
        cost_estimate=cost(),
    )(idx, x)


def times(chunks, panel, idx, base):
    m = len(chunks)
    counts = [len(pieces) for pieces in chunks]
    rows, w = sum(x.shape[0] for x in chunks[0]), chunks[0][0].shape[1]
    tile = min(256, rows // 2)
    steps = rows // tile

    def kernel(idx_ref, *refs):
        own, send, right = refs[-3:]
        pieces, rest = split(refs[:-3], counts)
        step = pl.program_id(0)

        @pl.when(step == 0)
        def _():
            for s in range(m):
                copy_block(right, s, rest, idx_ref[base + s], w)

        def block(refs):
            value = refs[0][...]
            for i in range(1, len(refs)):
                value = jnp.where(step // (steps // len(refs)) == i, refs[i][...], value)
            return value

        total = dot(jnp.concatenate([block(x) for x in pieces], axis=1), right[...])
        own[...] = total[:, :w]
        send[...] = total[:, w:].astype(BF16)

    def piece(part, count):
        each = steps // count
        return pl.BlockSpec((tile, w), lambda i, idx: (jnp.clip(i - part * each, 0, each - 1), 0))

    return pl.pallas_call(
        kernel,
        grid_spec=pltpu.PrefetchScalarGridSpec(
            num_scalar_prefetch=1,
            grid=(steps,),
            in_specs=[piece(part, count) for count in counts for part in range(count)]
            + [whole(x) for x in panel],
            out_specs=[pl.BlockSpec((tile, w), lambda i, idx: (i, 0))] * 2,
            scratch_shapes=[pltpu.VMEM((m * w, 2 * w), BF16)],
        ),
        out_shape=[
            jax.ShapeDtypeStruct((rows, w), F32),
            jax.ShapeDtypeStruct((rows, w), BF16),
        ],
        compiler_params=params(),
        cost_estimate=cost(),
    )(idx, *sum(chunks, []), *panel)


def load_all(chunks, held, sems):
    waits = []
    for s, pieces in enumerate(chunks):
        base, copies = 0, []
        for i, piece in enumerate(pieces):
            size = piece.shape[0]
            copies.append(
                pltpu.make_async_copy(piece, held.at[s, pl.ds(base, size)], sems.at[s, i])
            )
            copies[-1].start()
            base += size
        waits.append(copies)

    def wait(s):
        for copy in waits[s]:
            copy.wait()

    return wait


def split(refs, counts):
    out, base = [], 0
    for count in counts:
        out.append(list(refs[base : base + count]))
        base += count
    return out, refs[base:]


def times_t(chunks, right, idx, at0, form, start=(), hand_on=False, groups=()):
    m = len(chunks)
    counts = [len(pieces) for pieces in chunks]
    rows, w = sum(x.shape[0] for x in chunks[0]), chunks[0][0].shape[1]
    ANY = pl.BlockSpec(memory_space=pl.ANY)
    kept = lambda shape, dtype: jax.ShapeDtypeStruct(shape, dtype)
    if form == "blocks":
        outs = [kept((m * w, 2 * w), BF16)]
    elif form == "add":
        outs = [kept(x.shape, x.dtype) for x in start]
    else:
        outs = [kept((len(g) * w, w), t) for g in groups for t in (F32, F32, BF16, BF16)]
    blocks = [(4 * i, j) for i, g in enumerate(groups) for j, number in enumerate(g) for _ in range(number)]
    if hand_on:
        outs.append(kept((rows, 2 * w), BF16))

    def kernel(idx_ref, *refs):
        hbm, rest = split(refs, counts)
        right_refs, rest = rest[: len(right)], rest[len(right) :]
        start_refs, rest = rest[: len(start)], rest[len(start) :]
        out, (both, held, sems) = rest[: len(outs)], rest[len(outs) :]
        wait = load_all(hbm, held, sems)
        base = 0
        if len(right) == 1:
            both = right_refs[0]
        for j in range(0, len(right) - 1, 2):
            size = right[j].shape[0]
            both[base : base + size, :w] = right_refs[j][...]
            both[base : base + size, w:] = right_refs[j + 1][...]
            base += size
        for i in range(len(start)):
            out[i][...] = start_refs[i][...]
        if hand_on:
            out[-1][...] = both[...]
        for s in range(m):
            wait(s)
            value = dot_t(held[s], both[...])
            if form == "blocks":
                out[0][at(idx_ref[at0[s]], w), :] = value.astype(BF16)
            elif form == "add":
                place = at(idx_ref[at0[s]], w)
                out[0][place, :] = out[0][place, :] + value[:, :w]
                out[1][place, :] = (out[1][place, :].astype(F32) + value[:, w:]).astype(BF16)
            else:
                first, block = blocks[s]
                place = pl.ds(block * w, w)

                @pl.when(idx_ref[at0[s]] == 1)
                def _():
                    out[first][place, :] = value[:, :w]
                    out[first + 1][place, :] = value[:, w:]

                @pl.when(idx_ref[at0[s]] == 0)
                def _():
                    out[first + 2][place, :] = value[:, :w].astype(BF16)
                    out[first + 3][place, :] = value[:, w:].astype(BF16)

    return pl.pallas_call(
        kernel,
        grid_spec=pltpu.PrefetchScalarGridSpec(
            num_scalar_prefetch=1,
            grid=(1,),
            in_specs=[ANY] * sum(counts) + [whole(x) for x in (*right, *start)],
            out_specs=[whole(x) for x in outs],
            scratch_shapes=[
                pltpu.VMEM((rows if len(right) > 1 else 16, 2 * w), BF16),
                pltpu.VMEM((m, rows, w), BF16),
                pltpu.SemaphoreType.DMA((m, max(counts))),
            ],
        ),
        out_shape=outs,
        compiler_params=params(),
        cost_estimate=cost(4 * m * rows * w * w, 0),
    )(idx, *sum(chunks, []), *right, *start)


def finish(base, own, other, idx, core, places, so_far=None):
    w = base.shape[1]
    count = own[0].shape[0] // w

    def kernel(idx_ref, base_ref, a, b, c, d, *rest):
        k = idx_ref[core]
        for place, x, y in ((at(k, w), a, b), (at(1 - k, w), c, d)):
            value = x[...].astype(F32) + y[...].astype(F32)
            rest[-1][place, :] = (base_ref[place, :].astype(F32) - value).astype(BF16)

    here = pl.BlockSpec((2 * w, w), lambda t, idx: (idx[places + t], 0))
    extra = [] if so_far is None else [so_far]
    return pl.pallas_call(
        kernel,
        grid_spec=pltpu.PrefetchScalarGridSpec(
            num_scalar_prefetch=1,
            grid=(count,),
            in_specs=[here]
            + [pl.BlockSpec((w, w), lambda t, idx: (t, 0))] * 4
            + [pl.BlockSpec(memory_space=pl.ANY) for _ in extra],
            out_specs=here,
        ),
        out_shape=jax.ShapeDtypeStruct(base.shape, BF16),
        input_output_aliases={} if so_far is None else {6: 0},
        cost_estimate=cost(),
    )(idx, base, *own, *other, *extra)


def times_symmetric(chunks, panel, table, base0, slots):
    m = len(chunks)
    counts = [len(pieces) for pieces in chunks]
    w = chunks[0][0].shape[1]
    height = sum(x.shape[0] for x in panel) // 2
    inner = slots - 2
    half = w // 2
    ANY = pl.BlockSpec(memory_space=pl.ANY)

    def kernel(t, *refs):
        hbm, rest = split(refs, counts)
        panel_refs = rest[: len(panel)]
        own, send, acc, p, few, c, sems = rest[len(panel) :]
        wait = load_all(hbm, c, sems)
        base = 0
        for j in range(0, len(panel), 2):
            size = panel[j].shape[0]
            p[base : base + size, :w] = panel_refs[j][...]
            p[base : base + size, w:] = panel_refs[j + 1][...]
            base += size
        own[...] = jnp.zeros_like(own)
        acc[...] = jnp.zeros_like(acc)

        def add_at(place, value):
            own[place, :] = own[place, :] + value[:, :w]
            acc[place, :] = acc[place, :] + value[:, w:]

        def add(index, value):
            add_at(at(index, w), value)

        for s in range(m):
            b0 = base0 + s * (slots + 5)
            q = t[b0]
            row = lambda b: t[b0 + 1 + b]
            wait(s)
            right_q = p[at(q, w), :]
            for b in range(1, slots - 1):
                few[(b - 1) * w : b * w, :] = p[at(row(b), w), :]
            part = dot(c[s, : (slots - 1) * w, :], right_q)
            for b in range(slots - 1):
                add(row(b), part[b * w : (b + 1) * w])
            add(q, dot_t(c[s, w : (slots - 1) * w, :], few[...]))

            @pl.when(t[b0 + 3 + slots] == 1)
            def _():
                add(q, dot_t(c[s, :w, :], p[at(row(0), w), :]))

            @pl.when(t[b0 + 4 + slots] == 1)
            def _():
                last = c[s, (slots - 1) * w :, :]
                column = t[b0 + 1 + slots]
                place = at(2 * row(slots - 1) + t[b0 + 2 + slots], half)
                add_at(place, dot(last, p[at(column, w), :]))
                add(column, dot_t(last, p[place, :]))

        send[...] = acc[...].astype(BF16)

    return pl.pallas_call(
        kernel,
        grid_spec=pltpu.PrefetchScalarGridSpec(
            num_scalar_prefetch=1,
            grid=(1,),
            in_specs=[ANY] * sum(counts) + [whole(x) for x in panel],
            out_specs=[pl.BlockSpec((height, w), lambda i, t: (0, 0))] * 2,
            scratch_shapes=[
                pltpu.VMEM((height, w), F32),
                pltpu.VMEM((height, 2 * w), BF16),
                pltpu.VMEM((inner * w, 2 * w), BF16),
                pltpu.VMEM((m, (slots - 1) * w + half, w), BF16),
                pltpu.SemaphoreType.DMA((m, max(counts))),
            ],
        ),
        out_shape=[
            jax.ShapeDtypeStruct((height, w), F32),
            jax.ShapeDtypeStruct((height, w), BF16),
        ],
        compiler_params=params(),
        cost_estimate=cost(2 * height * height * w, 0),
    )(table, *sum(chunks, []), *panel)


def solution(mesh):
    R, C = mesh.shape["row"], mesh.shape["col"]
    n = C // 2
    nb = C // R
    slots = nb // 2 + 1
    order = list(range(0, n, 2)) + list(range(n - 1, 0, -2))
    place = [order.index(c) for c in range(n)]
    shifts = list(range(n))
    pairs = [(s, s + n // 2) for s in range(n // 2)]

    def ring_perm(shift):
        return [
            (c * 2 + k, order[(place[c] + shift) % n] * 2 + k) for c in range(n) for k in range(2)
        ]

    ring_perms = {1: ring_perm(1), -1: ring_perm(-1)}
    core_perm = [(i, i ^ 1) for i in range(C)]

    def slot(x, q):
        return ((q // nb) ^ x) * nb + q % nb if R == 2 else q

    def provided(x, q):
        h, lq = q // nb, q % nb
        if h == x:
            return [(lq + b) % nb for b in range(slots - 1)]
        return [(lq + 2 * b + (x > h)) % nb for b in range(slots - 1)]

    def sent(x, q):
        return provided(x, q) + [(q + nb // 2) % nb, int(q % nb >= nb // 2)]

    def rows_of(make):
        return np.array([[make(x, col) for col in range(C)] for x in range(R)], np.int32)

    def source(col, shift):
        return order[(place[col // 2] - shift) % n] * 2 + col % 2

    def symmetric_row(x, col):
        out = []
        for s in shifts:
            q = source(col, s)
            inside = q // nb == x
            out += [slot(x, q)] + [slot(x, x * nb + i) for i in provided(x, q)]
            low = q % nb % (nb // 2)
            out += [slot(x, x * nb + low + nb // 2), slot(x, x * nb + low)]
            out += [int(q % nb >= nb // 2), int(not inside), int(inside)]
        return out

    near, far = list(range(2, n // 2 - 1)), [1, n // 2 - 1]
    table_of = dict(
        send=sent,
        column=lambda x, col: [slot(x, source(col, s)) for s in shifts],
        chip=lambda x, col: [slot(x, source(col, s)) // 2 for s in shifts],
        symmetric=symmetric_row,
        mine=lambda x, col: [int(source(col, s) // nb == x) for s in shifts],
        places=lambda x, col: [
            max(source(col, s) % nb // 2 * int(source(col, s) // nb == x) for s in pairs[j])
            for j in near + far + [0]
        ],
        core=lambda x, col: [col % 2],
    )
    offsets, table = {}, []
    for name, make in table_of.items():
        rows = rows_of(make)
        offsets[name] = sum(x.shape[2] for x in table)
        table.append(rows)
    table = np.concatenate(table, axis=2)

    def core_swap(x):
        return lax.ppermute(x, "col", core_perm)

    def row_swap(x):
        return lax.ppermute(x, "row", [(0, 1), (1, 0)])

    def both_swap(x):
        pairs = [(x * C + i, (1 - x) * C + (i ^ 1)) for x in range(2) for i in range(C)]
        return lax.ppermute(x, ("row", "col"), pairs)

    def body(sigma, top_panel, top_dinv, low_upper, low_ancestor, low_dinv, low_rows):
        rows, w = sigma.shape
        r = lax.axis_index("row")
        col = lax.axis_index("col")
        k = col % 2
        index = lax.dynamic_slice(
            jnp.asarray(table), (r, col, 0), (1, 1, table.shape[2])
        ).reshape(-1)

        def gather_rows(x):
            if R == 2:
                return [x, row_swap(x)]
            return [lax.all_gather(x, "row", axis=0, tiled=True)]

        def both_cores(pieces):
            return [y for x in pieces for y in (x, core_swap(x))]

        def scatter_rows(x):
            if R == 2:
                half = x.shape[0] // 2
                return [x[:half], row_swap(x[half:].astype(BF16))]
            return [lax.psum_scatter(x.astype(BF16), "row", scatter_dimension=0, tiled=True)]

        def add(parts):
            return sum((x.astype(F32) for x in parts[1:]), parts[0].astype(F32))

        def own_columns(y):
            y = y.reshape(nb // 2, w, 2 * w)
            mine, theirs = y[..., :w], core_swap(y[..., w:])
            first = jnp.where(k == 0, mine, theirs)
            second = jnp.where(k == 0, theirs, mine)
            return jnp.stack([first, second], axis=1).reshape(rows, w)

        row_ids = (r * rows + jnp.arange(rows, dtype=jnp.int32)) // BLOCK
        in_pattern = jnp.any(row_ids[:, None] == low_rows[None, :], axis=1)[:, None]

        share = low_rows.shape[0] // R
        pattern_idx = lax.dynamic_slice_in_dim(low_rows, r * share, share)
        if R == 2:
            count = rows // BLOCK
            other_idx = lax.dynamic_slice_in_dim(low_rows, (1 - r) * share, share)
            pack_idx = jnp.concatenate([pattern_idx, other_idx]) % count
            pack_here = jnp.repeat(pattern_idx // count == r, BLOCK)[:, None]
        else:
            pack_idx = pattern_idx

        def take_pattern(x):
            return take_blocks(x, pack_idx, BLOCK) if R == 2 else x

        def pack_rows(taken):
            if R == 2:
                cut = share * BLOCK
                return [taken[:cut], row_swap(taken[cut:])]
            return [lax.all_gather(taken, "row", axis=0, tiled=True)]

        def packed(parts):
            if R == 2:
                return jnp.where(pack_here, *parts)
            return take_blocks(*parts, pattern_idx, BLOCK)

        steps = n // 2
        first = n - 1
        count = first + 3 * steps
        env, due, events = {}, {}, {}

        def step_of(stage, j):
            if stage == 0:
                return (j * (first - 1) + 2) // 3
            return first + (stage - 1) * steps + (j * (steps - 1) + 2) // 3

        def on(stage, j):
            def register(f):
                events.setdefault(step_of(stage, j), []).append(f)

            return register

        def keep(name, value, *until):
            env[name] = value
            if until:
                due[name] = step_of(*until)

        def ring_of(stage):
            return [env["ring", stage, s] for s in shifts]

        def entries(name, some=shifts):
            return [offsets[name] + s for s in some]

        def in_pairs(some):
            return [s for j in some for s in pairs[j]]

        def exchanged(own, other, rest_own, rest_other):
            return (own, row_swap(rest_own)), (core_swap(other), both_swap(rest_other))

        def finished(base, sums, first=0, so_far=None):
            place = offsets["places"] + first
            return finish(base, *sums, env["index"], offsets["core"], place, so_far)

        def core_sum(parts):
            own, send = parts
            return own + core_swap(send).astype(F32)

        @on(0, 0)
        def _():
            keep("upper_rows", gather_rows(low_upper), 0, 1)
            env["low_taken"] = take_pattern(low_ancestor)

        @on(0, 1)
        def _():
            keep("low_parts", pack_rows(env["low_taken"]), 0, 3)
            env["sigma_send"] = take_symmetric(sigma, env["index"], offsets["send"], slots)

        @on(0, 2)
        def _():
            keep("upper", both_cores(env["upper_rows"]), 0, 3)
            keep("top_rows", gather_rows(top_panel), 1, 0)
            env["dinv_send"] = take_symmetric(top_dinv, env["index"], offsets["send"], slots)

        @on(1, 1)
        def _():
            env["low_send"] = jnp.concatenate([low_upper, packed(env["low_parts"])], axis=0)

        @on(1, 0)
        def _():
            env["v_parts"] = times(ring_of(0), env["upper"], env["index"], offsets["column"])

        @on(1, 1)
        def _():
            own, send = env.pop("v_parts")
            env["v_parts"] = own, core_swap(send)

        @on(1, 2)
        def _():
            masked = jnp.where(in_pattern, low_ancestor, jnp.zeros_like(low_ancestor))
            v = (masked.astype(F32) - add(env.pop("v_parts"))).astype(BF16)
            keep("v_rows", gather_rows(v), 1, 3)

        @on(1, 3)
        def _():
            env["top_right"] = both_cores(env["top_rows"])

        @on(2, 0)
        def _():
            env["x_parts"] = times_symmetric(
                ring_of(1), both_cores(env["v_rows"]), env["index"], offsets["symmetric"], slots
            )

        @on(2, 1)
        def _():
            keep("x_sum", scatter_rows(core_sum(env.pop("x_parts"))), 2, 2)

        @on(2, 2)
        def _():
            env["off_parts"] = times_symmetric(
                ring_of(1), env["top_right"], env["index"], offsets["symmetric"], slots
            )

        @on(2, 3)
        def _():
            x = (-add(env.pop("x_sum"))).astype(BF16)
            env["low_anc"] = jnp.where(in_pattern, x, jnp.zeros_like(x))
            env["x"] = x
            keep("off_sum", scatter_rows(core_sum(env.pop("off_parts"))), 3, 0)

        @on(3, 0)
        def _():
            dinv_upper = times_symmetric(
                ring_of(2), env["upper"], env["index"], offsets["symmetric"], slots
            )
            env["low_top_parts"] = times_t(
                ring_of(0), both_cores([env["x"]]), env["index"], entries("column"), "add", dinv_upper
            )

        @on(3, 1)
        def _():
            keep("low_top_sum", scatter_rows(core_sum(env.pop("low_top_parts"))), 3, 1)
            env["x_taken"] = take_pattern(env["x"])
            env["top_off"] = (-add(env.pop("off_sum"))).astype(BF16)
            right = both_cores([env["top_off"]])
            if R == 2:
                at0 = entries("mine", in_pairs(near + far + [0]))
                chunks = [ring_of(0)[s] for s in in_pairs(near + far + [0])]
                groups = [[2] * len(pairs)]
                env["diag_parts"] = times_t(chunks, right, env["index"], at0, "pairs", groups=groups)
            else:
                env["diag_parts"] = times_t(ring_of(0), right, env["index"], entries("chip"), "blocks")

        @on(3, 2)
        def _():
            env["low_top"] = (-add(env.pop("low_top_sum"))).astype(BF16)
            env["low_top_both"] = both_cores([env["low_top"]])
            env["x_packed"] = both_cores([packed(pack_rows(env["x_taken"]))])
            if R == 2:
                keep("diag_sum", exchanged(*env.pop("diag_parts")), 3, 3)
            else:
                keep("diag_sum", scatter_rows(env.pop("diag_parts")[0]), 3, 3)

        def diag_part(some, groups, start=()):
            chunks = [env["ring", 3, s] for s in some]
            at0 = entries("mine", some)
            if "low_right" in env:
                right = [env["low_right"]]
                return times_t(chunks, right, env["index"], at0, "pairs", start, groups=groups)
            right = env["low_top_both"] + env["x_packed"]
            *out, env["low_right"] = times_t(
                chunks, right, env["index"], at0, "pairs", start, hand_on=True, groups=groups
            )
            return out

        if R == 2:

            @on(3, 2)
            def _():
                nearer = [1, n - 1, 0]
                some = in_pairs(near) + nearer
                out = diag_part(some, [[2] * len(near), [1, 1], [1]])
                env["near_parts"], env["far_parts"], env["last_parts"] = out[:4], out[4:8], out[8:]

            @on(3, 3)
            def _():
                keep("near", exchanged(*env.pop("near_parts")), 3, 3)
                env["top_diag"] = finished(top_dinv, env["diag_sum"])
                env["index"], _ = lax.optimization_barrier((env["index"], env["top_diag"]))
                farther = [steps + 1, steps - 1]
                env["far_parts"] = diag_part(farther, [[1, 1]], env["far_parts"])
                env["far"] = exchanged(*env["far_parts"])
                due["far"] = count

        env["index"] = index

        def hop(x, way):
            return lax.ppermute(x, "col", ring_perms[way])

        halves = list(jnp.split(top_panel, 2, axis=0))
        env["ring", 0, 0] = [top_panel]
        for s in shifts[1:]:
            env["ring", 0, s] = [None, None]
        flying = []

        def send_first(number):
            got = []
            for way in (1, -1):
                half, turn = (number + (way < 0)) % 2, number // 2
                x = env["ring", 0, way * turn % n][half] if turn else halves[half]
                got.append(((way * (turn + 1)) % n, half, hop(x, way)))
            flying.append(got)

        def send(stage, turn):
            if turn == 1:
                env["ring", stage, 0] = [env[("sigma_send", "dinv_send", "low_send")[stage - 1]]]
            held = [env["ring", stage, way * (turn - 1) % n][0] for way in (1, -1)]
            if turn == steps:
                half = held[0].shape[0] // 2
                held = [held[0][:half], held[1][half:]]
            got = [hop(x, way) for x, way in zip(held, (1, -1))]
            if turn == steps:
                return {("ring", stage, steps): got}
            return {("ring", stage, way * turn % n): [x] for x, way in zip(got, (1, -1))}

        send_first(0)
        for g in range(count):
            arriving = {}
            if g < first:
                if g + 1 < first:
                    send_first(g + 1)
            else:
                arriving = send((g - first) // steps + 1, (g - first) % steps + 1)
            for event in events.get(g, []):
                event()
            env.update(arriving)
            if g < first:
                for s, half, x in flying.pop(0):
                    env["ring", 0, s][half] = x
            names = [name for name in env if due.get(name, 0) <= g]
            leaves, tree = jax.tree.flatten([env[name] for name in names])
            env.update(zip(names, jax.tree.unflatten(tree, lax.optimization_barrier(leaves))))

        if R == 2:
            last = diag_part([steps], [[1]], env["last_parts"])
            low_diag = finished(low_dinv, env["near"])
            env["index"], _ = lax.optimization_barrier((env["index"], last[0]))
            last = exchanged(*last)
            low_diag = finished(low_dinv, env["far"], len(near), low_diag)
            low_diag = finished(low_dinv, last, len(near + far), low_diag)
            top_diag = env["top_diag"]
        else:
            right = env["low_top_both"] + env["x_packed"]
            parts = times_t(ring_of(3), right, env["index"], entries("chip"), "blocks")
            total = add(scatter_rows(parts[0]))
            low_diag = (low_dinv.astype(F32) - own_columns(total)).astype(BF16)
            top_diag = (top_dinv.astype(F32) - own_columns(add(env["diag_sum"]))).astype(BF16)
        return (env["top_off"], top_diag, env["low_top"], env["low_anc"], low_diag)

    spec = P("row", "col")
    return jax.shard_map(
        body, mesh=mesh, in_specs=(spec,) * 6 + (P(),), out_specs=(spec,) * 5, check_vma=False
    )
```

```python
import jax
import jax.numpy as jnp
import numpy as np
from jax import lax
from jax.experimental import pallas as pl
from jax.experimental.pallas import tpu as pltpu
from jax.sharding import PartitionSpec as P

BLOCK = 128
F32 = jnp.float32
BF16 = jnp.bfloat16
VMEM_BYTES = 56 * 1024 * 1024


def dot(a, b):
    return jnp.dot(a, b, preferred_element_type=F32)


def dot_t(a, b):
    return lax.dot_general(a, b, (((0,), (0,)), ((), ())), preferred_element_type=F32)


def cost(flops=0, bytes_accessed=0):
    return pl.CostEstimate(flops=1, bytes_accessed=1, transcendentals=0)


def params():
    return pltpu.CompilerParams(vmem_limit_bytes=VMEM_BYTES)


def at(index, size):
    return pl.ds(pl.multiple_of(index * size, size), size)


def whole(x):
    return pl.BlockSpec(x.shape, lambda i, idx: (0, 0))


def copy_block(out, place, panel, index, w):
    per = panel[0].shape[0] // w
    for j in range(0, len(panel), 2):

        @pl.when(index // per == j // 2)
        def _():
            rows = at(index - (j // 2) * per, w)
            out[pl.ds(place * w, w), :w] = panel[j][rows, :]
            out[pl.ds(place * w, w), w:] = panel[j + 1][rows, :]


def take_symmetric(x, idx, base, slots):
    w = x.shape[1]
    half = w // 2

    def kernel(idx_ref, x_ref, o_ref):
        for b in range(slots - 1):
            o_ref[b * w : (b + 1) * w, :] = x_ref[at(idx_ref[base + b], w), :]
        block = x_ref[at(idx_ref[base + slots - 1], w), :]
        turned = idx_ref[base + slots] == 1

        @pl.when(turned)
        def _():
            o_ref[(slots - 1) * w :, :] = block[:, half:].T

        @pl.when(jnp.logical_not(turned))
        def _():
            o_ref[(slots - 1) * w :, :] = block[:half, :]

    return pl.pallas_call(
        kernel,
        grid_spec=pltpu.PrefetchScalarGridSpec(
            num_scalar_prefetch=1,
            grid=(1,),
            in_specs=[whole(x)],
            out_specs=pl.BlockSpec(((slots - 1) * w + half, w), lambda i, idx: (0, 0)),
        ),
        out_shape=jax.ShapeDtypeStruct(((slots - 1) * w + half, w), x.dtype),
        cost_estimate=cost(),
    )(idx, x)


def take_blocks(x, idx, size):
    count, width = idx.shape[0], x.shape[1]

    def kernel(idx_ref, x_ref, o_ref):
        for i in range(count):
            o_ref[i * size : (i + 1) * size, :] = x_ref[at(idx_ref[i], size), :]

    return pl.pallas_call(
        kernel,
        grid_spec=pltpu.PrefetchScalarGridSpec(
            num_scalar_prefetch=1,
            grid=(1,),
            in_specs=[whole(x)],
            out_specs=pl.BlockSpec((count * size, width), lambda i, idx: (0, 0)),
        ),
        out_shape=jax.ShapeDtypeStruct((count * size, width), x.dtype),
        cost_estimate=cost(),
    )(idx, x)


def times(chunks, panel, idx, base):
    m = len(chunks)
    counts = [len(pieces) for pieces in chunks]
    rows, w = sum(x.shape[0] for x in chunks[0]), chunks[0][0].shape[1]
    tile = min(256, rows // 2)
    steps = rows // tile

    def kernel(idx_ref, *refs):
        own, send, right = refs[-3:]
        pieces, rest = split(refs[:-3], counts)
        step = pl.program_id(0)

        @pl.when(step == 0)
        def _():
            for s in range(m):
                copy_block(right, s, rest, idx_ref[base + s], w)

        def block(refs):
            value = refs[0][...]
            for i in range(1, len(refs)):
                value = jnp.where(step // (steps // len(refs)) == i, refs[i][...], value)
            return value

        total = dot(jnp.concatenate([block(x) for x in pieces], axis=1), right[...])
        own[...] = total[:, :w]
        send[...] = total[:, w:].astype(BF16)

    def piece(part, count):
        each = steps // count
        return pl.BlockSpec((tile, w), lambda i, idx: (jnp.clip(i - part * each, 0, each - 1), 0))

    return pl.pallas_call(
        kernel,
        grid_spec=pltpu.PrefetchScalarGridSpec(
            num_scalar_prefetch=1,
            grid=(steps,),
            in_specs=[piece(part, count) for count in counts for part in range(count)]
            + [whole(x) for x in panel],
            out_specs=[pl.BlockSpec((tile, w), lambda i, idx: (i, 0))] * 2,
            scratch_shapes=[pltpu.VMEM((m * w, 2 * w), BF16)],
        ),
        out_shape=[
            jax.ShapeDtypeStruct((rows, w), F32),
            jax.ShapeDtypeStruct((rows, w), BF16),
        ],
        compiler_params=params(),
        cost_estimate=cost(),
    )(idx, *sum(chunks, []), *panel)


def load_all(chunks, held, sems):
    waits = []
    for s, pieces in enumerate(chunks):
        base, copies = 0, []
        for i, piece in enumerate(pieces):
            size = piece.shape[0]
            copies.append(
                pltpu.make_async_copy(piece, held.at[s, pl.ds(base, size)], sems.at[s, i])
            )
            copies[-1].start()
            base += size
        waits.append(copies)

    def wait(s):
        for copy in waits[s]:
            copy.wait()

    return wait


def split(refs, counts):
    out, base = [], 0
    for count in counts:
        out.append(list(refs[base : base + count]))
        base += count
    return out, refs[base:]


def times_t(chunks, right, idx, at0, form, start=(), hand_on=False, groups=()):
    m = len(chunks)
    counts = [len(pieces) for pieces in chunks]
    rows, w = sum(x.shape[0] for x in chunks[0]), chunks[0][0].shape[1]
    ANY = pl.BlockSpec(memory_space=pl.ANY)
    kept = lambda shape, dtype: jax.ShapeDtypeStruct(shape, dtype)
    if form == "blocks":
        outs = [kept((m * w, 2 * w), BF16)]
    elif form == "add":
        outs = [kept(x.shape, x.dtype) for x in start]
    else:
        outs = [kept((len(g) * w, w), t) for g in groups for t in (F32, F32, BF16, BF16)]
    blocks = [(4 * i, j) for i, g in enumerate(groups) for j, number in enumerate(g) for _ in range(number)]
    if hand_on:
        outs.append(kept((rows, 2 * w), BF16))

    def kernel(idx_ref, *refs):
        hbm, rest = split(refs, counts)
        right_refs, rest = rest[: len(right)], rest[len(right) :]
        start_refs, rest = rest[: len(start)], rest[len(start) :]
        out, (both, held, sems) = rest[: len(outs)], rest[len(outs) :]
        wait = load_all(hbm, held, sems)
        base = 0
        if len(right) == 1:
            both = right_refs[0]
        for j in range(0, len(right) - 1, 2):
            size = right[j].shape[0]
            both[base : base + size, :w] = right_refs[j][...]
            both[base : base + size, w:] = right_refs[j + 1][...]
            base += size
        for i in range(len(start)):
            out[i][...] = start_refs[i][...]
        if hand_on:
            out[-1][...] = both[...]
        for s in range(m):
            wait(s)
            value = dot_t(held[s], both[...])
            if form == "blocks":
                out[0][at(idx_ref[at0[s]], w), :] = value.astype(BF16)
            elif form == "add":
                place = at(idx_ref[at0[s]], w)
                out[0][place, :] = out[0][place, :] + value[:, :w]
                out[1][place, :] = (out[1][place, :].astype(F32) + value[:, w:]).astype(BF16)
            else:
                first, block = blocks[s]
                place = pl.ds(block * w, w)

                @pl.when(idx_ref[at0[s]] == 1)
                def _():
                    out[first][place, :] = value[:, :w]
                    out[first + 1][place, :] = value[:, w:]

                @pl.when(idx_ref[at0[s]] == 0)
                def _():
                    out[first + 2][place, :] = value[:, :w].astype(BF16)
                    out[first + 3][place, :] = value[:, w:].astype(BF16)

    return pl.pallas_call(
        kernel,
        grid_spec=pltpu.PrefetchScalarGridSpec(
            num_scalar_prefetch=1,
            grid=(1,),
            in_specs=[ANY] * sum(counts) + [whole(x) for x in (*right, *start)],
            out_specs=[whole(x) for x in outs],
            scratch_shapes=[
                pltpu.VMEM((rows if len(right) > 1 else 16, 2 * w), BF16),
                pltpu.VMEM((m, rows, w), BF16),
                pltpu.SemaphoreType.DMA((m, max(counts))),
            ],
        ),
        out_shape=outs,
        compiler_params=params(),
        cost_estimate=cost(4 * m * rows * w * w, 0),
    )(idx, *sum(chunks, []), *right, *start)


def finish(base, own, other, idx, core, places, so_far=None):
    w = base.shape[1]
    count = own[0].shape[0] // w

    def kernel(idx_ref, base_ref, a, b, c, d, *rest):
        k = idx_ref[core]
        for place, x, y in ((at(k, w), a, b), (at(1 - k, w), c, d)):
            value = x[...].astype(F32) + y[...].astype(F32)
            rest[-1][place, :] = (base_ref[place, :].astype(F32) - value).astype(BF16)

    here = pl.BlockSpec((2 * w, w), lambda t, idx: (idx[places + t], 0))
    extra = [] if so_far is None else [so_far]
    return pl.pallas_call(
        kernel,
        grid_spec=pltpu.PrefetchScalarGridSpec(
            num_scalar_prefetch=1,
            grid=(count,),
            in_specs=[here]
            + [pl.BlockSpec((w, w), lambda t, idx: (t, 0))] * 4
            + [pl.BlockSpec(memory_space=pl.ANY) for _ in extra],
            out_specs=here,
        ),
        out_shape=jax.ShapeDtypeStruct(base.shape, BF16),
        input_output_aliases={} if so_far is None else {6: 0},
        cost_estimate=cost(),
    )(idx, base, *own, *other, *extra)


def times_symmetric(chunks, panel, table, base0, slots):
    m = len(chunks)
    counts = [len(pieces) for pieces in chunks]
    w = chunks[0][0].shape[1]
    height = sum(x.shape[0] for x in panel) // 2
    inner = slots - 2
    half = w // 2
    ANY = pl.BlockSpec(memory_space=pl.ANY)

    def kernel(t, *refs):
        hbm, rest = split(refs, counts)
        panel_refs = rest[: len(panel)]
        own, send, acc, p, few, c, sems = rest[len(panel) :]
        wait = load_all(hbm, c, sems)
        base = 0
        for j in range(0, len(panel), 2):
            size = panel[j].shape[0]
            p[base : base + size, :w] = panel_refs[j][...]
            p[base : base + size, w:] = panel_refs[j + 1][...]
            base += size
        own[...] = jnp.zeros_like(own)
        acc[...] = jnp.zeros_like(acc)

        def add_at(place, value):
            own[place, :] = own[place, :] + value[:, :w]
            acc[place, :] = acc[place, :] + value[:, w:]

        def add(index, value):
            add_at(at(index, w), value)

        for s in range(m):
            b0 = base0 + s * (slots + 5)
            q = t[b0]
            row = lambda b: t[b0 + 1 + b]
            wait(s)
            right_q = p[at(q, w), :]
            for b in range(1, slots - 1):
                few[(b - 1) * w : b * w, :] = p[at(row(b), w), :]
            part = dot(c[s, : (slots - 1) * w, :], right_q)
            for b in range(slots - 1):
                add(row(b), part[b * w : (b + 1) * w])
            add(q, dot_t(c[s, w : (slots - 1) * w, :], few[...]))

            @pl.when(t[b0 + 3 + slots] == 1)
            def _():
                add(q, dot_t(c[s, :w, :], p[at(row(0), w), :]))

            @pl.when(t[b0 + 4 + slots] == 1)
            def _():
                last = c[s, (slots - 1) * w :, :]
                column = t[b0 + 1 + slots]
                place = at(2 * row(slots - 1) + t[b0 + 2 + slots], half)
                add_at(place, dot(last, p[at(column, w), :]))
                add(column, dot_t(last, p[place, :]))

        send[...] = acc[...].astype(BF16)

    return pl.pallas_call(
        kernel,
        grid_spec=pltpu.PrefetchScalarGridSpec(
            num_scalar_prefetch=1,
            grid=(1,),
            in_specs=[ANY] * sum(counts) + [whole(x) for x in panel],
            out_specs=[pl.BlockSpec((height, w), lambda i, t: (0, 0))] * 2,
            scratch_shapes=[
                pltpu.VMEM((height, w), F32),
                pltpu.VMEM((height, 2 * w), BF16),
                pltpu.VMEM((inner * w, 2 * w), BF16),
                pltpu.VMEM((m, (slots - 1) * w + half, w), BF16),
                pltpu.SemaphoreType.DMA((m, max(counts))),
            ],
        ),
        out_shape=[
            jax.ShapeDtypeStruct((height, w), F32),
            jax.ShapeDtypeStruct((height, w), BF16),
        ],
        compiler_params=params(),
        cost_estimate=cost(2 * height * height * w, 0),
    )(table, *sum(chunks, []), *panel)


def solution(mesh):
    R, C = mesh.shape["row"], mesh.shape["col"]
    n = C // 2
    nb = C // R
    slots = nb // 2 + 1
    order = list(range(0, n, 2)) + list(range(n - 1, 0, -2))
    place = [order.index(c) for c in range(n)]
    shifts = list(range(n))
    pairs = [(s, s + n // 2) for s in range(n // 2)]

    def ring_perm(shift):
        return [
            (c * 2 + k, order[(place[c] + shift) % n] * 2 + k) for c in range(n) for k in range(2)
        ]

    ring_perms = {1: ring_perm(1), -1: ring_perm(-1)}
    core_perm = [(i, i ^ 1) for i in range(C)]

    def slot(x, q):
        return ((q // nb) ^ x) * nb + q % nb if R == 2 else q

    def provided(x, q):
        h, lq = q // nb, q % nb
        if h == x:
            return [(lq + b) % nb for b in range(slots - 1)]
        return [(lq + 2 * b + (x > h)) % nb for b in range(slots - 1)]

    def sent(x, q):
        return provided(x, q) + [(q + nb // 2) % nb, int(q % nb >= nb // 2)]

    def rows_of(make):
        return np.array([[make(x, col) for col in range(C)] for x in range(R)], np.int32)

    def source(col, shift):
        return order[(place[col // 2] - shift) % n] * 2 + col % 2

    def symmetric_row(x, col):
        out = []
        for s in shifts:
            q = source(col, s)
            inside = q // nb == x
            out += [slot(x, q)] + [slot(x, x * nb + i) for i in provided(x, q)]
            low = q % nb % (nb // 2)
            out += [slot(x, x * nb + low + nb // 2), slot(x, x * nb + low)]
            out += [int(q % nb >= nb // 2), int(not inside), int(inside)]
        return out

    near, far = list(range(2, n // 2 - 1)), [1, n // 2 - 1]
    table_of = dict(
        send=sent,
        column=lambda x, col: [slot(x, source(col, s)) for s in shifts],
        chip=lambda x, col: [slot(x, source(col, s)) // 2 for s in shifts],
        symmetric=symmetric_row,
        mine=lambda x, col: [int(source(col, s) // nb == x) for s in shifts],
        places=lambda x, col: [
            max(source(col, s) % nb // 2 * int(source(col, s) // nb == x) for s in pairs[j])
            for j in near + far + [0]
        ],
        core=lambda x, col: [col % 2],
    )
    offsets, table = {}, []
    for name, make in table_of.items():
        rows = rows_of(make)
        offsets[name] = sum(x.shape[2] for x in table)
        table.append(rows)
    table = np.concatenate(table, axis=2)

    def core_swap(x):
        return lax.ppermute(x, "col", core_perm)

    def row_swap(x):
        return lax.ppermute(x, "row", [(0, 1), (1, 0)])

    def both_swap(x):
        pairs = [(x * C + i, (1 - x) * C + (i ^ 1)) for x in range(2) for i in range(C)]
        return lax.ppermute(x, ("row", "col"), pairs)

    def body(sigma, top_panel, top_dinv, low_upper, low_ancestor, low_dinv, low_rows):
        rows, w = sigma.shape
        r = lax.axis_index("row")
        col = lax.axis_index("col")
        k = col % 2
        index = lax.dynamic_slice(
            jnp.asarray(table), (r, col, 0), (1, 1, table.shape[2])
        ).reshape(-1)

        def gather_rows(x):
            if R == 2:
                return [x, row_swap(x)]
            return [lax.all_gather(x, "row", axis=0, tiled=True)]

        def both_cores(pieces):
            return [y for x in pieces for y in (x, core_swap(x))]

        def scatter_rows(x):
            if R == 2:
                half = x.shape[0] // 2
                return [x[:half], row_swap(x[half:].astype(BF16))]
            return [lax.psum_scatter(x.astype(BF16), "row", scatter_dimension=0, tiled=True)]

        def add(parts):
            return sum((x.astype(F32) for x in parts[1:]), parts[0].astype(F32))

        def own_columns(y):
            y = y.reshape(nb // 2, w, 2 * w)
            mine, theirs = y[..., :w], core_swap(y[..., w:])
            first = jnp.where(k == 0, mine, theirs)
            second = jnp.where(k == 0, theirs, mine)
            return jnp.stack([first, second], axis=1).reshape(rows, w)

        row_ids = (r * rows + jnp.arange(rows, dtype=jnp.int32)) // BLOCK
        in_pattern = jnp.any(row_ids[:, None] == low_rows[None, :], axis=1)[:, None]

        share = low_rows.shape[0] // R
        pattern_idx = lax.dynamic_slice_in_dim(low_rows, r * share, share)
        if R == 2:
            count = rows // BLOCK
            other_idx = lax.dynamic_slice_in_dim(low_rows, (1 - r) * share, share)
            pack_idx = jnp.concatenate([pattern_idx, other_idx]) % count
            pack_here = jnp.repeat(pattern_idx // count == r, BLOCK)[:, None]
        else:
            pack_idx = pattern_idx

        def take_pattern(x):
            return take_blocks(x, pack_idx, BLOCK) if R == 2 else x

        def pack_rows(taken):
            if R == 2:
                cut = share * BLOCK
                return [taken[:cut], row_swap(taken[cut:])]
            return [lax.all_gather(taken, "row", axis=0, tiled=True)]

        def packed(parts):
            if R == 2:
                return jnp.where(pack_here, *parts)
            return take_blocks(*parts, pattern_idx, BLOCK)

        steps = n // 2
        first = n - 1
        count = first + 3 * steps
        env, due, events = {}, {}, {}

        def step_of(stage, j):
            if stage == 0:
                return (j * (first - 1) + 2) // 3
            return first + (stage - 1) * steps + (j * (steps - 1) + 2) // 3

        def on(stage, j):
            def register(f):
                events.setdefault(step_of(stage, j), []).append(f)

            return register

        def keep(name, value, *until):
            env[name] = value
            if until:
                due[name] = step_of(*until)

        def ring_of(stage):
            return [env["ring", stage, s] for s in shifts]

        def entries(name, some=shifts):
            return [offsets[name] + s for s in some]

        def in_pairs(some):
            return [s for j in some for s in pairs[j]]

        def exchanged(own, other, rest_own, rest_other):
            return (own, row_swap(rest_own)), (core_swap(other), both_swap(rest_other))

        def finished(base, sums, first=0, so_far=None):
            place = offsets["places"] + first
            return finish(base, *sums, env["index"], offsets["core"], place, so_far)

        def core_sum(parts):
            own, send = parts
            return own + core_swap(send).astype(F32)

        @on(0, 0)
        def _():
            keep("upper_rows", gather_rows(low_upper), 0, 1)
            env["low_taken"] = take_pattern(low_ancestor)

        @on(0, 1)
        def _():
            keep("low_parts", pack_rows(env["low_taken"]), 0, 3)
            env["sigma_send"] = take_symmetric(sigma, env["index"], offsets["send"], slots)

        @on(0, 2)
        def _():
            keep("upper", both_cores(env["upper_rows"]), 0, 3)
            keep("top_rows", gather_rows(top_panel), 1, 0)
            env["dinv_send"] = take_symmetric(top_dinv, env["index"], offsets["send"], slots)

        @on(1, 1)
        def _():
            env["low_send"] = jnp.concatenate([low_upper, packed(env["low_parts"])], axis=0)

        @on(1, 0)
        def _():
            env["v_parts"] = times(ring_of(0), env["upper"], env["index"], offsets["column"])

        @on(1, 1)
        def _():
            own, send = env.pop("v_parts")
            env["v_parts"] = own, core_swap(send)

        @on(1, 2)
        def _():
            masked = jnp.where(in_pattern, low_ancestor, jnp.zeros_like(low_ancestor))
            v = (masked.astype(F32) - add(env.pop("v_parts"))).astype(BF16)
            keep("v_rows", gather_rows(v), 1, 3)

        @on(1, 3)
        def _():
            env["top_right"] = both_cores(env["top_rows"])

        @on(2, 0)
        def _():
            env["x_parts"] = times_symmetric(
                ring_of(1), both_cores(env["v_rows"]), env["index"], offsets["symmetric"], slots
            )

        @on(2, 1)
        def _():
            keep("x_sum", scatter_rows(core_sum(env.pop("x_parts"))), 2, 2)

        @on(2, 2)
        def _():
            env["off_parts"] = times_symmetric(
                ring_of(1), env["top_right"], env["index"], offsets["symmetric"], slots
            )

        @on(2, 3)
        def _():
            x = (-add(env.pop("x_sum"))).astype(BF16)
            env["low_anc"] = jnp.where(in_pattern, x, jnp.zeros_like(x))
            env["x"] = x
            keep("off_sum", scatter_rows(core_sum(env.pop("off_parts"))), 3, 0)

        @on(3, 0)
        def _():
            dinv_upper = times_symmetric(
                ring_of(2), env["upper"], env["index"], offsets["symmetric"], slots
            )
            env["low_top_parts"] = times_t(
                ring_of(0), both_cores([env["x"]]), env["index"], entries("column"), "add", dinv_upper
            )

        @on(3, 1)
        def _():
            own, other = env.pop("low_top_parts")
            other = core_swap(other)
            off_sum, _ = lax.optimization_barrier((env.pop("off_sum"), other))
            keep("low_top_sum", scatter_rows(add([own, other])), 3, 1)
            env["x_taken"] = take_pattern(env["x"])
            env["top_off"] = (-add(off_sum)).astype(BF16)
            right = both_cores([env["top_off"]])
            if R == 2:
                at0 = entries("mine", in_pairs(near + far + [0]))
                chunks = [ring_of(0)[s] for s in in_pairs(near + far + [0])]
                groups = [[2] * len(pairs)]
                env["diag_parts"] = times_t(chunks, right, env["index"], at0, "pairs", groups=groups)
            else:
                env["diag_parts"] = times_t(ring_of(0), right, env["index"], entries("chip"), "blocks")

        @on(3, 2)
        def _():
            env["low_top"] = (-add(env.pop("low_top_sum"))).astype(BF16)
            env["low_top_both"] = both_cores([env["low_top"]])
            env["x_packed"] = both_cores([packed(pack_rows(env["x_taken"]))])
            if R == 2:
                keep("diag_sum", exchanged(*env.pop("diag_parts")), 3, 3)
            else:
                keep("diag_sum", scatter_rows(env.pop("diag_parts")[0]), 3, 3)

        def diag_part(some, groups, start=()):
            chunks = [env["ring", 3, s] for s in some]
            at0 = entries("mine", some)
            if "low_right" in env:
                right = [env["low_right"]]
                return times_t(chunks, right, env["index"], at0, "pairs", start, groups=groups)
            right = env["low_top_both"] + env["x_packed"]
            *out, env["low_right"] = times_t(
                chunks, right, env["index"], at0, "pairs", start, hand_on=True, groups=groups
            )
            return out

        if R == 2:

            @on(3, 2)
            def _():
                nearer = [1, n - 1, 0]
                some = in_pairs(near) + nearer
                out = diag_part(some, [[2] * len(near), [1, 1], [1]])
                env["near_parts"], env["far_parts"], env["last_parts"] = out[:4], out[4:8], out[8:]

            @on(3, 3)
            def _():
                keep("near", exchanged(*env.pop("near_parts")), 3, 3)
                env["top_diag"] = finished(top_dinv, env["diag_sum"])
                env["index"], _ = lax.optimization_barrier((env["index"], env["top_diag"]))
                farther = [steps + 1, steps - 1]
                env["far_parts"] = diag_part(farther, [[1, 1]], env["far_parts"])
                env["far"] = exchanged(*env["far_parts"])
                due["far"] = count

        env["index"] = index

        def hop(x, way):
            return lax.ppermute(x, "col", ring_perms[way])

        halves = list(jnp.split(top_panel, 2, axis=0))
        env["ring", 0, 0] = [top_panel]
        for s in shifts[1:]:
            env["ring", 0, s] = [None, None]
        flying = []

        def send_first(number):
            got = []
            for way in (1, -1):
                half, turn = (number + (way < 0)) % 2, number // 2
                x = env["ring", 0, way * turn % n][half] if turn else halves[half]
                got.append(((way * (turn + 1)) % n, half, hop(x, way)))
            flying.append(got)

        def send(stage, turn):
            if turn == 1:
                env["ring", stage, 0] = [env[("sigma_send", "dinv_send", "low_send")[stage - 1]]]
            held = [env["ring", stage, way * (turn - 1) % n][0] for way in (1, -1)]
            if turn == steps:
                half = held[0].shape[0] // 2
                held = [held[0][:half], held[1][half:]]
            got = [hop(x, way) for x, way in zip(held, (1, -1))]
            if turn == steps:
                return {("ring", stage, steps): got}
            return {("ring", stage, way * turn % n): [x] for x, way in zip(got, (1, -1))}

        send_first(0)
        for g in range(count):
            arriving = {}
            if g < first:
                if g + 1 < first:
                    send_first(g + 1)
            else:
                arriving = send((g - first) // steps + 1, (g - first) % steps + 1)
            for event in events.get(g, []):
                event()
            env.update(arriving)
            if g < first:
                for s, half, x in flying.pop(0):
                    env["ring", 0, s][half] = x
            names = [name for name in env if due.get(name, 0) <= g]
            leaves, tree = jax.tree.flatten([env[name] for name in names])
            env.update(zip(names, jax.tree.unflatten(tree, lax.optimization_barrier(leaves))))

        if R == 2:
            last = diag_part([steps], [[1]], env["last_parts"])
            low_diag = finished(low_dinv, env["near"])
            env["index"], _ = lax.optimization_barrier((env["index"], last[0]))
            last = exchanged(*last)
            low_diag = finished(low_dinv, env["far"], len(near), low_diag)
            low_diag = finished(low_dinv, last, len(near + far), low_diag)
            top_diag = env["top_diag"]
        else:
            right = env["low_top_both"] + env["x_packed"]
            parts = times_t(ring_of(3), right, env["index"], entries("chip"), "blocks")
            total = add(scatter_rows(parts[0]))
            low_diag = (low_dinv.astype(F32) - own_columns(total)).astype(BF16)
            top_diag = (top_dinv.astype(F32) - own_columns(add(env["diag_sum"]))).astype(BF16)
        return (env["top_off"], top_diag, env["low_top"], env["low_anc"], low_diag)

    spec = P("row", "col")
    return jax.shard_map(
        body, mesh=mesh, in_specs=(spec,) * 6 + (P(),), out_specs=(spec,) * 5, check_vma=False
    )
```

```python
import jax
import jax.numpy as jnp
import numpy as np
from jax import lax
from jax.experimental import pallas as pl
from jax.experimental.pallas import tpu as pltpu
from jax.sharding import PartitionSpec as P

BLOCK = 128
F32 = jnp.float32
BF16 = jnp.bfloat16
VMEM_BYTES = 56 * 1024 * 1024


def dot(a, b):
    return jnp.dot(a, b, preferred_element_type=F32)


def dot_t(a, b):
    return lax.dot_general(a, b, (((0,), (0,)), ((), ())), preferred_element_type=F32)


def cost(flops=0, bytes_accessed=0):
    return pl.CostEstimate(flops=1, bytes_accessed=1, transcendentals=0)


def params():
    return pltpu.CompilerParams(vmem_limit_bytes=VMEM_BYTES)


def at(index, size):
    return pl.ds(pl.multiple_of(index * size, size), size)


def whole(x):
    return pl.BlockSpec(x.shape, lambda i, idx: (0, 0))


def copy_block(out, place, panel, index, w):
    per = panel[0].shape[0] // w
    for j in range(0, len(panel), 2):

        @pl.when(index // per == j // 2)
        def _():
            rows = at(index - (j // 2) * per, w)
            out[pl.ds(place * w, w), :w] = panel[j][rows, :]
            out[pl.ds(place * w, w), w:] = panel[j + 1][rows, :]


def take_symmetric(x, idx, base, slots):
    w = x.shape[1]
    half = w // 2

    def kernel(idx_ref, x_ref, o_ref):
        for b in range(slots - 1):
            o_ref[b * w : (b + 1) * w, :] = x_ref[at(idx_ref[base + b], w), :]
        block = x_ref[at(idx_ref[base + slots - 1], w), :]
        turned = idx_ref[base + slots] == 1

        @pl.when(turned)
        def _():
            o_ref[(slots - 1) * w :, :] = block[:, half:].T

        @pl.when(jnp.logical_not(turned))
        def _():
            o_ref[(slots - 1) * w :, :] = block[:half, :]

    return pl.pallas_call(
        kernel,
        grid_spec=pltpu.PrefetchScalarGridSpec(
            num_scalar_prefetch=1,
            grid=(1,),
            in_specs=[whole(x)],
            out_specs=pl.BlockSpec(((slots - 1) * w + half, w), lambda i, idx: (0, 0)),
        ),
        out_shape=jax.ShapeDtypeStruct(((slots - 1) * w + half, w), x.dtype),
        cost_estimate=cost(),
    )(idx, x)


def take_blocks(x, idx, size):
    count, width = idx.shape[0], x.shape[1]

    def kernel(idx_ref, x_ref, o_ref):
        for i in range(count):
            o_ref[i * size : (i + 1) * size, :] = x_ref[at(idx_ref[i], size), :]

    return pl.pallas_call(
        kernel,
        grid_spec=pltpu.PrefetchScalarGridSpec(
            num_scalar_prefetch=1,
            grid=(1,),
            in_specs=[whole(x)],
            out_specs=pl.BlockSpec((count * size, width), lambda i, idx: (0, 0)),
        ),
        out_shape=jax.ShapeDtypeStruct((count * size, width), x.dtype),
        cost_estimate=cost(),
    )(idx, x)


def times(chunks, panel, idx, base):
    m = len(chunks)
    counts = [len(pieces) for pieces in chunks]
    rows, w = sum(x.shape[0] for x in chunks[0]), chunks[0][0].shape[1]
    tile = min(256, rows // 2)
    steps = rows // tile

    def kernel(idx_ref, *refs):
        own, send, right = refs[-3:]
        pieces, rest = split(refs[:-3], counts)
        step = pl.program_id(0)

        @pl.when(step == 0)
        def _():
            for s in range(m):
                copy_block(right, s, rest, idx_ref[base + s], w)

        def block(refs):
            value = refs[0][...]
            for i in range(1, len(refs)):
                value = jnp.where(step // (steps // len(refs)) == i, refs[i][...], value)
            return value

        total = dot(jnp.concatenate([block(x) for x in pieces], axis=1), right[...])
        own[...] = total[:, :w]
        send[...] = total[:, w:].astype(BF16)

    def piece(part, count):
        each = steps // count
        return pl.BlockSpec((tile, w), lambda i, idx: (jnp.clip(i - part * each, 0, each - 1), 0))

    return pl.pallas_call(
        kernel,
        grid_spec=pltpu.PrefetchScalarGridSpec(
            num_scalar_prefetch=1,
            grid=(steps,),
            in_specs=[piece(part, count) for count in counts for part in range(count)]
            + [whole(x) for x in panel],
            out_specs=[pl.BlockSpec((tile, w), lambda i, idx: (i, 0))] * 2,
            scratch_shapes=[pltpu.VMEM((m * w, 2 * w), BF16)],
        ),
        out_shape=[
            jax.ShapeDtypeStruct((rows, w), F32),
            jax.ShapeDtypeStruct((rows, w), BF16),
        ],
        compiler_params=params(),
        cost_estimate=cost(),
    )(idx, *sum(chunks, []), *panel)


def load_all(chunks, held, sems):
    waits = []
    for s, pieces in enumerate(chunks):
        base, copies = 0, []
        for i, piece in enumerate(pieces):
            size = piece.shape[0]
            copies.append(
                pltpu.make_async_copy(piece, held.at[s, pl.ds(base, size)], sems.at[s, i])
            )
            copies[-1].start()
            base += size
        waits.append(copies)

    def wait(s):
        for copy in waits[s]:
            copy.wait()

    return wait


def split(refs, counts):
    out, base = [], 0
    for count in counts:
        out.append(list(refs[base : base + count]))
        base += count
    return out, refs[base:]


def times_t(chunks, right, idx, at0, form, start=(), hand_on=False, groups=()):
    m = len(chunks)
    counts = [len(pieces) for pieces in chunks]
    rows, w = sum(x.shape[0] for x in chunks[0]), chunks[0][0].shape[1]
    ANY = pl.BlockSpec(memory_space=pl.ANY)
    kept = lambda shape, dtype: jax.ShapeDtypeStruct(shape, dtype)
    if form == "blocks":
        outs = [kept((m * w, 2 * w), BF16)]
    elif form == "add":
        outs = [kept(x.shape, x.dtype) for x in start]
    else:
        outs = [kept((len(g) * w, w), t) for g in groups for t in (F32, F32, BF16, BF16)]
    blocks = [(4 * i, j) for i, g in enumerate(groups) for j, number in enumerate(g) for _ in range(number)]
    if hand_on:
        outs.append(kept((rows, 2 * w), BF16))

    def kernel(idx_ref, *refs):
        hbm, rest = split(refs, counts)
        right_refs, rest = rest[: len(right)], rest[len(right) :]
        start_refs, rest = rest[: len(start)], rest[len(start) :]
        out, (both, held, sems) = rest[: len(outs)], rest[len(outs) :]
        wait = load_all(hbm, held, sems)
        base = 0
        if len(right) == 1:
            both = right_refs[0]
        for j in range(0, len(right) - 1, 2):
            size = right[j].shape[0]
            both[base : base + size, :w] = right_refs[j][...]
            both[base : base + size, w:] = right_refs[j + 1][...]
            base += size
        for i in range(len(start)):
            out[i][...] = start_refs[i][...]
        if hand_on:
            out[-1][...] = both[...]
        for s in range(m):
            wait(s)
            value = dot_t(held[s], both[...])
            if form == "blocks":
                out[0][at(idx_ref[at0[s]], w), :] = value.astype(BF16)
            elif form == "add":
                place = at(idx_ref[at0[s]], w)
                out[0][place, :] = out[0][place, :] + value[:, :w]
                out[1][place, :] = (out[1][place, :].astype(F32) + value[:, w:]).astype(BF16)
            else:
                first, block = blocks[s]
                place = pl.ds(block * w, w)

                @pl.when(idx_ref[at0[s]] == 1)
                def _():
                    out[first][place, :] = value[:, :w]
                    out[first + 1][place, :] = value[:, w:]

                @pl.when(idx_ref[at0[s]] == 0)
                def _():
                    out[first + 2][place, :] = value[:, :w].astype(BF16)
                    out[first + 3][place, :] = value[:, w:].astype(BF16)

    return pl.pallas_call(
        kernel,
        grid_spec=pltpu.PrefetchScalarGridSpec(
            num_scalar_prefetch=1,
            grid=(1,),
            in_specs=[ANY] * sum(counts) + [whole(x) for x in (*right, *start)],
            out_specs=[whole(x) for x in outs],
            scratch_shapes=[
                pltpu.VMEM((rows if len(right) > 1 else 16, 2 * w), BF16),
                pltpu.VMEM((m, rows, w), BF16),
                pltpu.SemaphoreType.DMA((m, max(counts))),
            ],
        ),
        out_shape=outs,
        compiler_params=params(),
        cost_estimate=cost(4 * m * rows * w * w, 0),
    )(idx, *sum(chunks, []), *right, *start)


def finish(base, own, other, idx, core, places, so_far=None):
    w = base.shape[1]
    count = own[0].shape[0] // w

    def kernel(idx_ref, base_ref, a, b, c, d, *rest):
        k = idx_ref[core]
        for place, x, y in ((at(k, w), a, b), (at(1 - k, w), c, d)):
            value = x[...].astype(F32) + y[...].astype(F32)
            rest[-1][place, :] = (base_ref[place, :].astype(F32) - value).astype(BF16)

    here = pl.BlockSpec((2 * w, w), lambda t, idx: (idx[places + t], 0))
    extra = [] if so_far is None else [so_far]
    return pl.pallas_call(
        kernel,
        grid_spec=pltpu.PrefetchScalarGridSpec(
            num_scalar_prefetch=1,
            grid=(count,),
            in_specs=[here]
            + [pl.BlockSpec((w, w), lambda t, idx: (t, 0))] * 4
            + [pl.BlockSpec(memory_space=pl.ANY) for _ in extra],
            out_specs=here,
        ),
        out_shape=jax.ShapeDtypeStruct(base.shape, BF16),
        input_output_aliases={} if so_far is None else {6: 0},
        cost_estimate=cost(),
    )(idx, base, *own, *other, *extra)


def times_symmetric(chunks, panel, table, base0, slots):
    m = len(chunks)
    counts = [len(pieces) for pieces in chunks]
    w = chunks[0][0].shape[1]
    height = sum(x.shape[0] for x in panel) // 2
    inner = slots - 2
    half = w // 2
    ANY = pl.BlockSpec(memory_space=pl.ANY)

    def kernel(t, *refs):
        hbm, rest = split(refs, counts)
        panel_refs = rest[: len(panel)]
        own, send, acc, p, few, c, sems = rest[len(panel) :]
        wait = load_all(hbm, c, sems)
        base = 0
        for j in range(0, len(panel), 2):
            size = panel[j].shape[0]
            p[base : base + size, :w] = panel_refs[j][...]
            p[base : base + size, w:] = panel_refs[j + 1][...]
            base += size
        own[...] = jnp.zeros_like(own)
        acc[...] = jnp.zeros_like(acc)

        def add_at(place, value):
            own[place, :] = own[place, :] + value[:, :w]
            acc[place, :] = acc[place, :] + value[:, w:]

        def add(index, value):
            add_at(at(index, w), value)

        for s in range(m):
            b0 = base0 + s * (slots + 5)
            q = t[b0]
            row = lambda b: t[b0 + 1 + b]
            wait(s)
            right_q = p[at(q, w), :]
            for b in range(1, slots - 1):
                few[(b - 1) * w : b * w, :] = p[at(row(b), w), :]
            part = dot(c[s, : (slots - 1) * w, :], right_q)
            for b in range(slots - 1):
                add(row(b), part[b * w : (b + 1) * w])
            add(q, dot_t(c[s, w : (slots - 1) * w, :], few[...]))

            @pl.when(t[b0 + 3 + slots] == 1)
            def _():
                add(q, dot_t(c[s, :w, :], p[at(row(0), w), :]))

            @pl.when(t[b0 + 4 + slots] == 1)
            def _():
                last = c[s, (slots - 1) * w :, :]
                column = t[b0 + 1 + slots]
                place = at(2 * row(slots - 1) + t[b0 + 2 + slots], half)
                add_at(place, dot(last, p[at(column, w), :]))
                add(column, dot_t(last, p[place, :]))

        send[...] = acc[...].astype(BF16)

    return pl.pallas_call(
        kernel,
        grid_spec=pltpu.PrefetchScalarGridSpec(
            num_scalar_prefetch=1,
            grid=(1,),
            in_specs=[ANY] * sum(counts) + [whole(x) for x in panel],
            out_specs=[pl.BlockSpec((height, w), lambda i, t: (0, 0))] * 2,
            scratch_shapes=[
                pltpu.VMEM((height, w), F32),
                pltpu.VMEM((height, 2 * w), BF16),
                pltpu.VMEM((inner * w, 2 * w), BF16),
                pltpu.VMEM((m, (slots - 1) * w + half, w), BF16),
                pltpu.SemaphoreType.DMA((m, max(counts))),
            ],
        ),
        out_shape=[
            jax.ShapeDtypeStruct((height, w), F32),
            jax.ShapeDtypeStruct((height, w), BF16),
        ],
        compiler_params=params(),
        cost_estimate=cost(2 * height * height * w, 0),
    )(table, *sum(chunks, []), *panel)


def solution(mesh):
    R, C = mesh.shape["row"], mesh.shape["col"]
    n = C // 2
    nb = C // R
    slots = nb // 2 + 1
    order = list(range(0, n, 2)) + list(range(n - 1, 0, -2))
    place = [order.index(c) for c in range(n)]
    shifts = list(range(n))
    pairs = [(s, s + n // 2) for s in range(n // 2)]

    def ring_perm(shift):
        return [
            (c * 2 + k, order[(place[c] + shift) % n] * 2 + k) for c in range(n) for k in range(2)
        ]

    ring_perms = {1: ring_perm(1), -1: ring_perm(-1)}
    core_perm = [(i, i ^ 1) for i in range(C)]

    def slot(x, q):
        return ((q // nb) ^ x) * nb + q % nb if R == 2 else q

    def provided(x, q):
        h, lq = q // nb, q % nb
        if h == x:
            return [(lq + b) % nb for b in range(slots - 1)]
        return [(lq + 2 * b + (x > h)) % nb for b in range(slots - 1)]

    def sent(x, q):
        return provided(x, q) + [(q + nb // 2) % nb, int(q % nb >= nb // 2)]

    def rows_of(make):
        return np.array([[make(x, col) for col in range(C)] for x in range(R)], np.int32)

    def source(col, shift):
        return order[(place[col // 2] - shift) % n] * 2 + col % 2

    def symmetric_row(x, col):
        out = []
        for s in shifts:
            q = source(col, s)
            inside = q // nb == x
            out += [slot(x, q)] + [slot(x, x * nb + i) for i in provided(x, q)]
            low = q % nb % (nb // 2)
            out += [slot(x, x * nb + low + nb // 2), slot(x, x * nb + low)]
            out += [int(q % nb >= nb // 2), int(not inside), int(inside)]
        return out

    near, far = list(range(2, n // 2 - 1)), [1, n // 2 - 1]
    table_of = dict(
        send=sent,
        column=lambda x, col: [slot(x, source(col, s)) for s in shifts],
        chip=lambda x, col: [slot(x, source(col, s)) // 2 for s in shifts],
        symmetric=symmetric_row,
        mine=lambda x, col: [int(source(col, s) // nb == x) for s in shifts],
        places=lambda x, col: [
            max(source(col, s) % nb // 2 * int(source(col, s) // nb == x) for s in pairs[j])
            for j in near + far + [0]
        ],
        core=lambda x, col: [col % 2],
    )
    offsets, table = {}, []
    for name, make in table_of.items():
        rows = rows_of(make)
        offsets[name] = sum(x.shape[2] for x in table)
        table.append(rows)
    table = np.concatenate(table, axis=2)

    def core_swap(x):
        return lax.ppermute(x, "col", core_perm)

    def row_swap(x):
        return lax.ppermute(x, "row", [(0, 1), (1, 0)])

    def both_swap(x):
        pairs = [(x * C + i, (1 - x) * C + (i ^ 1)) for x in range(2) for i in range(C)]
        return lax.ppermute(x, ("row", "col"), pairs)

    def body(sigma, top_panel, top_dinv, low_upper, low_ancestor, low_dinv, low_rows):
        rows, w = sigma.shape
        r = lax.axis_index("row")
        col = lax.axis_index("col")
        k = col % 2
        index = lax.dynamic_slice(
            jnp.asarray(table), (r, col, 0), (1, 1, table.shape[2])
        ).reshape(-1)

        def gather_rows(x):
            if R == 2:
                return [x, row_swap(x)]
            return [lax.all_gather(x, "row", axis=0, tiled=True)]

        def both_cores(pieces):
            return [y for x in pieces for y in (x, core_swap(x))]

        def scatter_rows(x):
            if R == 2:
                half = x.shape[0] // 2
                return [x[:half], row_swap(x[half:].astype(BF16))]
            return [lax.psum_scatter(x.astype(BF16), "row", scatter_dimension=0, tiled=True)]

        def add(parts):
            return sum((x.astype(F32) for x in parts[1:]), parts[0].astype(F32))

        def own_columns(y):
            y = y.reshape(nb // 2, w, 2 * w)
            mine, theirs = y[..., :w], core_swap(y[..., w:])
            first = jnp.where(k == 0, mine, theirs)
            second = jnp.where(k == 0, theirs, mine)
            return jnp.stack([first, second], axis=1).reshape(rows, w)

        row_ids = (r * rows + jnp.arange(rows, dtype=jnp.int32)) // BLOCK
        in_pattern = jnp.any(row_ids[:, None] == low_rows[None, :], axis=1)[:, None]

        share = low_rows.shape[0] // R
        pattern_idx = lax.dynamic_slice_in_dim(low_rows, r * share, share)
        if R == 2:
            count = rows // BLOCK
            other_idx = lax.dynamic_slice_in_dim(low_rows, (1 - r) * share, share)
            pack_idx = jnp.concatenate([pattern_idx, other_idx]) % count
            pack_here = jnp.repeat(pattern_idx // count == r, BLOCK)[:, None]
        else:
            pack_idx = pattern_idx

        def take_pattern(x):
            return take_blocks(x, pack_idx, BLOCK) if R == 2 else x

        def pack_rows(taken):
            if R == 2:
                cut = share * BLOCK
                return [taken[:cut], row_swap(taken[cut:])]
            return [lax.all_gather(taken, "row", axis=0, tiled=True)]

        def packed(parts):
            if R == 2:
                return jnp.where(pack_here, *parts)
            return take_blocks(*parts, pattern_idx, BLOCK)

        steps = n // 2
        first = n - 1
        count = first + 3 * steps
        env, due, events = {}, {}, {}

        def step_of(stage, j):
            if stage == 0:
                return (j * (first - 1) + 2) // 3
            return first + (stage - 1) * steps + (j * (steps - 1) + 2) // 3

        def on(stage, j):
            def register(f):
                events.setdefault(step_of(stage, j), []).append(f)

            return register

        def keep(name, value, *until):
            env[name] = value
            if until:
                due[name] = step_of(*until)

        def ring_of(stage):
            return [env["ring", stage, s] for s in shifts]

        def entries(name, some=shifts):
            return [offsets[name] + s for s in some]

        def in_pairs(some):
            return [s for j in some for s in pairs[j]]

        def exchanged(own, other, rest_own, rest_other):
            return (own, row_swap(rest_own)), (core_swap(other), both_swap(rest_other))

        def finished(base, sums, first=0, so_far=None):
            place = offsets["places"] + first
            return finish(base, *sums, env["index"], offsets["core"], place, so_far)

        def core_sum(parts):
            own, send = parts
            return own + core_swap(send).astype(F32)

        @on(0, 0)
        def _():
            keep("upper_rows", gather_rows(low_upper), 0, 1)
            env["low_taken"] = take_pattern(low_ancestor)

        @on(0, 1)
        def _():
            keep("low_parts", pack_rows(env["low_taken"]), 0, 3)
            env["sigma_send"] = take_symmetric(sigma, env["index"], offsets["send"], slots)

        @on(0, 2)
        def _():
            keep("upper", both_cores(env["upper_rows"]), 0, 3)
            keep("top_rows", gather_rows(top_panel), 1, 0)

        @on(1, 1)
        def _():
            env["dinv_send"] = take_symmetric(top_dinv, env["index"], offsets["send"], slots)
            env["low_send"] = jnp.concatenate([low_upper, packed(env["low_parts"])], axis=0)

        @on(1, 0)
        def _():
            env["v_parts"] = times(ring_of(0), env["upper"], env["index"], offsets["column"])

        @on(1, 1)
        def _():
            own, send = env.pop("v_parts")
            env["v_parts"] = own, core_swap(send)

        @on(1, 2)
        def _():
            masked = jnp.where(in_pattern, low_ancestor, jnp.zeros_like(low_ancestor))
            v = (masked.astype(F32) - add(env.pop("v_parts"))).astype(BF16)
            keep("v_rows", gather_rows(v), 1, 3)

        @on(1, 3)
        def _():
            env["top_right"] = both_cores(env["top_rows"])

        @on(2, 0)
        def _():
            env["x_parts"] = times_symmetric(
                ring_of(1), both_cores(env["v_rows"]), env["index"], offsets["symmetric"], slots
            )

        @on(2, 1)
        def _():
            keep("x_sum", scatter_rows(core_sum(env.pop("x_parts"))), 2, 2)

        @on(2, 2)
        def _():
            env["off_parts"] = times_symmetric(
                ring_of(1), env["top_right"], env["index"], offsets["symmetric"], slots
            )

        @on(2, 3)
        def _():
            x = (-add(env.pop("x_sum"))).astype(BF16)
            env["low_anc"] = jnp.where(in_pattern, x, jnp.zeros_like(x))
            env["x"] = x
            keep("off_sum", scatter_rows(core_sum(env.pop("off_parts"))), 3, 0)

        @on(3, 0)
        def _():
            dinv_upper = times_symmetric(
                ring_of(2), env["upper"], env["index"], offsets["symmetric"], slots
            )
            env["low_top_parts"] = times_t(
                ring_of(0), both_cores([env["x"]]), env["index"], entries("column"), "add", dinv_upper
            )

        @on(3, 1)
        def _():
            own, other = env.pop("low_top_parts")
            other = core_swap(other)
            off_sum, _ = lax.optimization_barrier((env.pop("off_sum"), other))
            keep("low_top_sum", scatter_rows(add([own, other])), 3, 1)
            env["x_taken"] = take_pattern(env["x"])
            env["top_off"] = (-add(off_sum)).astype(BF16)
            right = both_cores([env["top_off"]])
            if R == 2:
                at0 = entries("mine", in_pairs(near + far + [0]))
                chunks = [ring_of(0)[s] for s in in_pairs(near + far + [0])]
                groups = [[2] * len(pairs)]
                env["diag_parts"] = times_t(chunks, right, env["index"], at0, "pairs", groups=groups)
            else:
                env["diag_parts"] = times_t(ring_of(0), right, env["index"], entries("chip"), "blocks")

        @on(3, 2)
        def _():
            env["low_top"] = (-add(env.pop("low_top_sum"))).astype(BF16)
            env["low_top_both"] = both_cores([env["low_top"]])
            env["x_packed"] = both_cores([packed(pack_rows(env["x_taken"]))])
            if R == 2:
                keep("diag_sum", exchanged(*env.pop("diag_parts")), 3, 3)
            else:
                keep("diag_sum", scatter_rows(env.pop("diag_parts")[0]), 3, 3)

        def diag_part(some, groups, start=()):
            chunks = [env["ring", 3, s] for s in some]
            at0 = entries("mine", some)
            if "low_right" in env:
                right = [env["low_right"]]
                return times_t(chunks, right, env["index"], at0, "pairs", start, groups=groups)
            right = env["low_top_both"] + env["x_packed"]
            *out, env["low_right"] = times_t(
                chunks, right, env["index"], at0, "pairs", start, hand_on=True, groups=groups
            )
            return out

        if R == 2:

            @on(3, 2)
            def _():
                nearer = [1, n - 1, 0]
                some = in_pairs(near) + nearer
                out = diag_part(some, [[2] * len(near), [1, 1], [1]])
                env["near_parts"], env["far_parts"], env["last_parts"] = out[:4], out[4:8], out[8:]

            @on(3, 3)
            def _():
                keep("near", exchanged(*env.pop("near_parts")), 3, 3)
                env["top_diag"] = finished(top_dinv, env["diag_sum"])
                env["index"], _ = lax.optimization_barrier((env["index"], env["top_diag"]))
                farther = [steps + 1, steps - 1]
                env["far_parts"] = diag_part(farther, [[1, 1]], env["far_parts"])
                env["far"] = exchanged(*env["far_parts"])
                due["far"] = count

        env["index"] = index

        def hop(x, way):
            return lax.ppermute(x, "col", ring_perms[way])

        halves = list(jnp.split(top_panel, 2, axis=0))
        env["ring", 0, 0] = [top_panel]
        for s in shifts[1:]:
            env["ring", 0, s] = [None, None]
        flying = []

        def send_first(number):
            got = []
            for way in (1, -1):
                half, turn = (number + (way < 0)) % 2, number // 2
                x = env["ring", 0, way * turn % n][half] if turn else halves[half]
                got.append(((way * (turn + 1)) % n, half, hop(x, way)))
            flying.append(got)

        def send(stage, turn):
            if turn == 1:
                env["ring", stage, 0] = [env[("sigma_send", "dinv_send", "low_send")[stage - 1]]]
            held = [env["ring", stage, way * (turn - 1) % n][0] for way in (1, -1)]
            if turn == steps:
                half = held[0].shape[0] // 2
                held = [held[0][:half], held[1][half:]]
            got = [hop(x, way) for x, way in zip(held, (1, -1))]
            if turn == steps:
                return {("ring", stage, steps): got}
            return {("ring", stage, way * turn % n): [x] for x, way in zip(got, (1, -1))}

        send_first(0)
        for g in range(count):
            arriving = {}
            if g < first:
                if g + 1 < first:
                    send_first(g + 1)
            else:
                arriving = send((g - first) // steps + 1, (g - first) % steps + 1)
            for event in events.get(g, []):
                event()
            env.update(arriving)
            if g < first:
                for s, half, x in flying.pop(0):
                    env["ring", 0, s][half] = x
            names = [name for name in env if due.get(name, 0) <= g]
            leaves, tree = jax.tree.flatten([env[name] for name in names])
            env.update(zip(names, jax.tree.unflatten(tree, lax.optimization_barrier(leaves))))

        if R == 2:
            last = diag_part([steps], [[1]], env["last_parts"])
            low_diag = finished(low_dinv, env["near"])
            env["index"], _ = lax.optimization_barrier((env["index"], last[0]))
            last = exchanged(*last)
            low_diag = finished(low_dinv, env["far"], len(near), low_diag)
            low_diag = finished(low_dinv, last, len(near + far), low_diag)
            top_diag = env["top_diag"]
        else:
            right = env["low_top_both"] + env["x_packed"]
            parts = times_t(ring_of(3), right, env["index"], entries("chip"), "blocks")
            total = add(scatter_rows(parts[0]))
            low_diag = (low_dinv.astype(F32) - own_columns(total)).astype(BF16)
            top_diag = (top_dinv.astype(F32) - own_columns(add(env["diag_sum"]))).astype(BF16)
        return (env["top_off"], top_diag, env["low_top"], env["low_anc"], low_diag)

    spec = P("row", "col")
    return jax.shard_map(
        body, mesh=mesh, in_specs=(spec,) * 6 + (P(),), out_specs=(spec,) * 5, check_vma=False
    )
```
